128 devices in a mesh: section: 2 (over core), fsdp: 64 (over z, x, y).
Axes of the slice: x: 4, y: 4, z: 4, core: 2. Of those that a mesh axis runs over, the one named last changes fastest.
Arguments:
- tokens: bfloat16 [8192, 896], P('fsdp'), may hold values from -6 to 6
- segments: int32 [8192], P('fsdp'), may hold values from 0 to 3, as said below
- cotangent: bfloat16 [8192, 896], P('fsdp'), may hold values from -6 to 6
- w_qkv: bfloat16 [2, 896, 1152], P('section', 'fsdp'), may hold values from -0.1875 to 0.1875
- b_qkv: bfloat16 [2, 1152], P('section', 'fsdp'), may hold values from -3 to 3
- w_out: bfloat16 [2, 896, 896], P('section', 'fsdp'), may hold values from -0.75 to 0.75
- gain_attn: bfloat16 [2, 896], P('section', 'fsdp'), may hold values from 0.5 to 1.5
- gain_mlp: bfloat16 [2, 896], P('section', 'fsdp'), may hold values from 0.5 to 1.5
- w_gate: bfloat16 [2, 896, 4864], P('section', 'fsdp'), may hold values from -0.1875 to 0.1875
- w_up: bfloat16 [2, 896, 4864], P('section', 'fsdp'), may hold values from -0.1875 to 0.1875
- w_down: bfloat16 [2, 4864, 896], P('section', 'fsdp'), may hold values from -0.078125 to 0.078125
Outputs:
- states: bfloat16 [2, 8192, 896], P('section', 'fsdp')
- input_grads: float32 [2, 8192, 896], P('section', 'fsdp')
- grad_w_qkv: float32 [2, 896, 1152], P('section', 'fsdp')
- grad_b_qkv: float32 [2, 1152], P('section', 'fsdp')
- grad_w_out: float32 [2, 896, 896], P('section', 'fsdp')
- grad_gain_attn: float32 [2, 896], P('section', 'fsdp')
- grad_gain_mlp: float32 [2, 896], P('section', 'fsdp')
- grad_w_gate: float32 [2, 896, 4864], P('section', 'fsdp')
- grad_w_up: float32 [2, 896, 4864], P('section', 'fsdp')
- grad_w_down: float32 [2, 4864, 896], P('section', 'fsdp')
The draws below stay inside these ranges and needn't reach their ends.
Inputs may be any that keep to these rules, and one draw needn't show every extreme that they name: `segments`: within each block of 64 tokens the ids start at 0 and never fall; a block holds one to four sequences, and the number differs between blocks; block 0 holds four, block 1 one.
All inputs are finite; a program needn't handle non-finite values.
Results may differ from the reference program's by a relative error of at most 0.018.
Values may be sent and summed in bfloat16 or wider, within the bound.
A program may use at most 512 MiB of HBM per device.

```python
import jax
import jax.numpy as jnp
from jax import lax

D = 896
QH = 14
KVH = 2
HD = 64
FF = 4864
QKV = 1152
ROWS = 64
TOKENS = 8192


def draw_segments(key, part):
    key = jax.random.fold_in(key, 7)
    blocks = TOKENS // ROWS
    key_count, key_place = jax.random.split(key)
    number = jax.random.randint(key_count, (blocks,), 0, 4)
    number = number.at[0].set(3).at[1].set(0)
    third = ROWS // 3
    offsets = jax.random.randint(key_place, (blocks, 3), 1, third)
    cuts = offsets + jnp.arange(3, dtype=jnp.int32)[None, :] * third
    index = jnp.arange(ROWS, dtype=jnp.int32)
    active = jnp.arange(3, dtype=jnp.int32)[None, :] < number[:, None]
    crossed = (index[None, None, :] >= cuts[:, :, None]) & active[:, :, None]
    return jnp.sum(crossed.astype(jnp.int32), axis=1).reshape(TOKENS).astype(jnp.int32)


def shard_levels(key, extent, cuts, least, largest):
    loudness = 1.0
    for position, parts in cuts:
        steps = jax.random.uniform(jax.random.fold_in(jax.random.fold_in(key, 6), position), (parts,), jnp.float32, least / len(cuts), largest / len(cuts))
        loudness = loudness * jnp.repeat(jnp.exp(steps), extent[position] // parts).reshape((-1,) + (1,) * (len(extent) - 1 - position))
    return loudness


def scatter_about(rng, shape, width, bound, cuts=(), kind=jnp.bfloat16):
    entries = width * jax.random.normal(rng, shape, jnp.float32)
    if cuts:
        entries = entries * shard_levels(rng, shape, cuts, -0.22, 0.18)
    return jnp.clip(entries, -bound, bound).astype(kind)


def setup_inputs(seed: int = 0) -> dict:
    streams_of = jax.random.split(jax.random.key(seed), 12)
    return {
        "tokens": scatter_about(streams_of[0], (TOKENS, D), 1.0, 6.0, ((0, 64),)),
        "segments": draw_segments(jax.random.fold_in(streams_of[11], 71), 0),
        "cotangent": scatter_about(streams_of[2], (TOKENS, D), 1.0, 6.0, ((0, 64),)),
        "w_qkv": scatter_about(streams_of[3], (2, D, QKV), D ** -0.5, 0.1875, ((0, 2), (1, 64))),
        "b_qkv": scatter_about(streams_of[4], (2, QKV), 0.5, 3.0, ((0, 2), (1, 64))),
        "w_out": scatter_about(streams_of[5], (2, D, D), (D // 16) ** -0.5, 0.75, ((0, 2), (1, 64))),
        "gain_attn": jnp.clip(1.0 + 0.1 * jax.random.normal(streams_of[6], (2, D), jnp.float32), 0.5, 1.5).astype(jnp.bfloat16),
        "gain_mlp": jnp.clip(1.0 + 0.1 * jax.random.normal(streams_of[7], (2, D), jnp.float32), 0.5, 1.5).astype(jnp.bfloat16),
        "w_gate": scatter_about(streams_of[8], (2, D, FF), D ** -0.5, 0.1875, ((0, 2), (1, 64))),
        "w_up": scatter_about(streams_of[9], (2, D, FF), D ** -0.5, 0.1875, ((0, 2), (1, 64))),
        "w_down": scatter_about(streams_of[10], (2, FF, D), FF ** -0.5, 0.078125, ((0, 2), (1, 64))),
    }


@jax.custom_vjp
def low(v):
    return lax.optimization_barrier(v.astype(jnp.bfloat16)).astype(jnp.float32)

@jax.custom_vjp
def low_back(v):
    return v

def low_keep(v):
    return (low(v), None)

def low_pass(kept, grad):
    return (grad,)

def back_keep(v):
    return (v, None)

def back_low(kept, grad):
    return (low(grad),)
low.defvjp(low_keep, low_pass)
low_back.defvjp(back_keep, back_low)
eps_norm = 1e-06
theta_base = 1000000.0

def matmul_high(left, right):
    return jnp.dot(left, right, precision=lax.Precision.HIGHEST)

def rotation(segment):
    index = jnp.arange(segment.shape[0], dtype=jnp.int32)
    earlier = lax.optimization_barrier(jnp.sum((segment[None, :] < segment[:, None]).astype(jnp.int32), axis=1)).astype(jnp.int32)
    place = (index - earlier).astype(jnp.float32)
    half = HD // 2
    inverse = theta_base ** (-(jnp.arange(half, dtype=jnp.float32) * 2.0 / HD))
    angles = place[:, None] * inverse[None, :]
    return (jnp.cos(angles), jnp.sin(angles))

def rotate(values, cosine, sine):
    half = HD // 2
    first = values[..., :half]
    second = values[..., half:]
    cosine = cosine[:, None, :]
    sine = sine[:, None, :]
    return jnp.concatenate([first * cosine - second * sine, second * cosine + first * sine], axis=-1)

def rms_norm(stream, gain):
    inverse = lax.rsqrt(lax.optimization_barrier(jnp.mean(stream * stream, axis=-1, keepdims=True)) + eps_norm)
    return stream * inverse * gain

def layer_block(stream, segment, params):
    w_qkv, b_qkv, w_out, gain_attn, gain_mlp, w_gate, w_up, w_down = params
    rows = stream.shape[0]
    normed = low(rms_norm(stream, gain_attn))
    projected = low_back(matmul_high(normed, w_qkv) + b_qkv)
    cosine, sine = rotation(segment)
    queries = low(rotate(projected[:, :QH * HD].reshape(rows, QH, HD), cosine, sine))
    keys = low(rotate(projected[:, QH * HD:QH * HD + KVH * HD].reshape(rows, KVH, HD), cosine, sine))
    values = low(projected[:, QH * HD + KVH * HD:].reshape(rows, KVH, HD))
    grouped = queries.reshape(rows, KVH, QH // KVH, HD)
    scores = jnp.einsum('rkgd,skd->kgrs', grouped, keys, precision=lax.Precision.HIGHEST) * HD ** (-0.5)
    scores = low_back(scores)
    index = jnp.arange(rows)
    allowed = (segment[:, None] == segment[None, :]) & (index[None, :] <= index[:, None])
    masked = jnp.where(allowed, scores, -1e+30)
    top = lax.optimization_barrier(jnp.max(masked, axis=-1, keepdims=True))
    weights = jnp.exp(masked - top)
    probs = low(weights / lax.optimization_barrier(jnp.sum(weights, axis=-1, keepdims=True)))
    mixed = jnp.einsum('kgrs,skd->rkgd', probs, values, precision=lax.Precision.HIGHEST).reshape(rows, QH * HD)
    mixed = low_back(low(mixed))
    middle = stream + low_back(matmul_high(mixed, w_out))
    normed_mlp = low(rms_norm(middle, gain_mlp))
    gate = low_back(matmul_high(normed_mlp, w_gate))
    upward = low_back(matmul_high(normed_mlp, w_up))
    active = low(jax.nn.silu(gate) * upward)
    return middle + low_back(matmul_high(active, w_down))

def reference(tokens, segments, cotangent, w_qkv, b_qkv, w_out, gain_attn, gain_mlp, w_gate, w_up, w_down):
    blocks = TOKENS // ROWS
    seg_blocks = segments.reshape(blocks, ROWS)
    params = tuple((item.astype(jnp.float32) for item in (w_qkv, b_qkv, w_out, gain_attn, gain_mlp, w_gate, w_up, w_down)))
    stream = tokens.astype(jnp.float32).reshape(blocks, ROWS, D)
    shift_in = jnp.zeros((blocks, ROWS, D), jnp.float32)

    def forward(stream_in, shift_value, params_all):
        layer_zero = tuple((item[0] for item in params_all))
        layer_one = tuple((item[1] for item in params_all))

        def run_zero(block, segment):
            return layer_block(block, segment, layer_zero)

        def run_one(block, segment):
            return layer_block(block, segment, layer_one)
        middle = low(jax.vmap(run_zero)(stream_in, seg_blocks))
        passed = low_back(middle + shift_value)
        final = jax.vmap(run_one)(passed, seg_blocks)
        return (final, middle)
    final, vjp_fn, middle = jax.vjp(forward, stream, shift_in, params, has_aux=True)
    grad_stream, grad_shift, grad_params = vjp_fn(cotangent.astype(jnp.float32).reshape(blocks, ROWS, D))
    states = jnp.stack([middle.reshape(TOKENS, D), final.reshape(TOKENS, D)]).astype(jnp.bfloat16)
    input_grads = jnp.stack([grad_stream.reshape(TOKENS, D), grad_shift.reshape(TOKENS, D)])
    return (states, input_grads, grad_params[0], grad_params[1], grad_params[2], grad_params[3], grad_params[4], grad_params[5], grad_params[6], grad_params[7])
```

```python
import functools

import jax
import jax.numpy as jnp
import numpy as np
from jax import lax
from jax.experimental import pallas as pl
from jax.experimental.pallas import tpu as pltpu
from jax.sharding import PartitionSpec as P

D = 896
QH = 14
KVH = 2
HD = 64
FF = 4864
QKV = 1152
ROWS = 64
TOK = 128
RING = 4

DP = 1024
FP = 1280
ATT = QKV + DP
N_SEM = 96

eps_norm = 1e-06
theta_base = 1000000.0
MESH = pl.DeviceIdType.MESH
F32 = jnp.float32
BF16 = jnp.bfloat16


def dot(left, right):
    return jnp.dot(left, right, preferred_element_type=F32)


def dot_back(left, right):
    return lax.dot_general(left, right, (((1,), (1,)), ((), ())), preferred_element_type=F32)


def dot_rows(left, right):
    return lax.dot_general(left, right, (((0,), (0,)), ((), ())), preferred_element_type=F32)


def times(n, step):
    def run(i, carry):
        step(i)
        return carry

    lax.fori_loop(0, n, run, 0)


def span(start, size, unit):
    return pl.ds(pl.multiple_of(start, unit), size)


def kernel(
    tok, cot, cos_t, sin_t, mask, gu_in, d_in, qkv_in, out_in, pad_s,
    states, igrads, ogu, od, oqkv, oout,
    w_att, w_gu, w_d, g_att,
    xin, dyin, ybuf, dxbuf, h1, obuf, do_buf, datt, dp_buf,
    h2all, dmall, gact, aact, dgu, h2t, at,
    part_f, part_b, af1, af2, ab1, ab2, dh,
    u1, u2, x1, proj, qs, kd, vd, probs,
    zg1, zg2, xg1, xg2, yg, xd1, xd2, zd1, zd2, ya1, ya2, xa1, xa2, za1, za2,
    send, recv,
):
    sec = lax.axis_index("section")
    me = lax.axis_index("fsdp")
    z, x, y = me // 16, lax.rem(me // 4, 4), lax.rem(me, 4)
    up1 = lambda c: lax.rem(c + 1, RING)
    up2 = lambda c: lax.rem(c + 2, RING)
    up3 = lambda c: lax.rem(c + 3, RING)

    def at_z(c):
        return (sec, c * 16 + x * 4 + y)

    def at_x(c):
        return (sec, z * 16 + c * 4 + y)

    def at_y(c):
        return (sec, z * 16 + x * 4 + c)

    other = (1 - sec, me)
    barrier = pltpu.get_barrier_semaphore()
    partners = [
        at_z(up1(z)), at_z(up3(z)), at_x(up1(x)), at_x(up3(x)),
        at_y(up1(y)), at_y(up3(y)), at_y(up2(y)), other,
    ]
    for dev in partners:
        pl.semaphore_signal(barrier, inc=1, device_id=dev, device_id_type=MESH)

    count = [0]
    pending = []

    def remote(src, dst, dev):
        k = count[0]
        count[0] += 1
        cp = pltpu.make_async_remote_copy(
            src_ref=src, dst_ref=dst, send_sem=send.at[k], recv_sem=recv.at[k],
            device_id=dev, device_id_type=MESH,
        )
        return cp

    def go(src, dst, dev):
        cp = remote(src, dst, dev)
        cp.start()
        pending.append(cp)
        return cp

    class Gather:
        def __init__(self, blk, low, high, c, dev):
            self.blk, self.low, self.high, self.c, self.dev = blk, low, high, c, dev

        def start(self):
            c = self.c
            self.a = go(self.blk(c), self.blk(c), self.dev(up1(c)))
            self.b = go(self.blk(c), self.blk(c), self.dev(up3(c)))

        def mid(self):
            c = self.c
            self.a.wait_recv()
            self.e = go(self.low(up3(c)), self.low(up3(c)), self.dev(up1(c)))
            self.b.wait_recv()
            self.f = go(self.high(up1(c)), self.high(up1(c)), self.dev(up3(c)))

        def end(self):
            self.e.wait_recv()
            self.f.wait_recv()

    class Reduce:
        def __init__(self, blk, low, high, c, dev, r1, r2, add):
            self.blk, self.low, self.high, self.c, self.dev = blk, low, high, c, dev
            self.r1, self.r2, self.add = r1, r2, add

        def start(self):
            c = self.c
            self.a = go(self.low(up2(c)), self.r1.at[0], self.dev(up1(c)))
            self.b = go(self.high(up2(c)), self.r1.at[1], self.dev(up3(c)))

        def mid(self):
            c = self.c
            self.a.wait_recv()
            self.add(up1(c), 0, self.r1.at[0])
            self.e = go(self.blk(up1(c)), self.r2.at[0], self.dev(up1(c)))
            self.b.wait_recv()
            self.add(up3(c), 1, self.r1.at[1])
            self.f = go(self.blk(up3(c)), self.r2.at[1], self.dev(up3(c)))

        def end(self):
            self.e.wait_recv()
            self.f.wait_recv()

    mine_d = span(320 * x + 80 * z, 80, 16)
    mine_gu = span(256 * z + 64 * x + 16 * y, 16, 16)
    w_d[mine_d, :] = dot(d_in[...], pad_s[...]).astype(BF16)
    w_gu[mine_gu, :] = gu_in[y]
    w_att[z, x, y, :, :QKV] = qkv_in[...]
    w_att[z, x, y, :, QKV:] = dot(out_in[...], pad_s[...]).astype(BF16)
    pl.semaphore_wait(barrier, len(partners))

    gu_copies = []
    for step in (up1, up3, up2):
        gu_copies.append(go(gu_in.at[step(y)], w_gu.at[mine_gu], at_y(step(y))))
    att_z = Gather(
        lambda c: w_att.at[c, x, y],
        lambda c: w_att.at[c, x, y, :, pl.ds(0, QKV)],
        lambda c: w_att.at[c, x, y, :, pl.ds(QKV, DP)], z, at_z)
    att_x = Gather(
        lambda c: w_att.at[:, c, y],
        lambda c: w_att.at[:, c, y, :, pl.ds(0, QKV)],
        lambda c: w_att.at[:, c, y, :, pl.ds(QKV, DP)], x, at_x)
    att_y = Gather(
        lambda c: w_att.at[:, :, c],
        lambda c: w_att.at[:, :, c, :, pl.ds(0, QKV)],
        lambda c: w_att.at[:, :, c, :, pl.ds(QKV, DP)], y, at_y)
    gu_x = Gather(
        lambda c: w_gu.at[span(256 * z + 64 * c, 64, 64)],
        lambda c: w_gu.at[span(256 * z + 64 * c, 64, 64), pl.ds(0, FP)],
        lambda c: w_gu.at[span(256 * z + 64 * c, 64, 64), pl.ds(FP, FP)], x, at_x)
    gu_z = Gather(
        lambda c: w_gu.at[span(256 * c, 256, 256)],
        lambda c: w_gu.at[span(256 * c, 256, 256), pl.ds(0, FP)],
        lambda c: w_gu.at[span(256 * c, 256, 256), pl.ds(FP, FP)], z, at_z)
    d_z = Gather(
        lambda c: w_d.at[span(320 * x + 80 * c, 80, 16)],
        lambda c: w_d.at[span(320 * x + 80 * c, 80, 16), pl.ds(0, 512)],
        lambda c: w_d.at[span(320 * x + 80 * c, 80, 16), pl.ds(512, 512)], z, at_z)
    d_x = Gather(
        lambda c: w_d.at[span(320 * c, 320, 64)],
        lambda c: w_d.at[span(320 * c, 320, 64), pl.ds(0, 512)],
        lambda c: w_d.at[span(320 * c, 320, 64), pl.ds(512, 512)], x, at_x)
    att_z.start()
    d_z.start()
    for cp in gu_copies:
        cp.wait_recv()
    gu_x.start()
    att_z.mid()
    d_z.mid()
    gu_x.mid()
    att_z.end()
    att_x.start()
    gu_x.end()
    gu_z.start()
    d_z.end()
    d_x.start()
    att_x.mid()
    att_x.end()
    att_y.start()
    d_x.mid()
    att_y.mid()
    att_y.end()

    send_y = remote(ybuf, xin, other)
    send_dx = remote(dxbuf, dyin, other)

    @pl.when(sec == 0)
    def _():
        xin[...] = dot(tok[...], pad_s[...]).astype(BF16)

    @pl.when(sec == 1)
    def _():
        dyin[...] = dot(cot[...], pad_s[...]).astype(BF16)

    gu_z.mid()
    d_x.end()
    gu_z.end()

    @pl.when(sec == 1)
    def _():
        send_y.wait_recv()

    lanes = lax.broadcasted_iota(jnp.int32, (TOK, DP), 1)
    slot = lax.rem(lanes, 16)
    picks = lax.broadcasted_iota(jnp.int32, (8, DP), 1)
    pick15 = jnp.where(lax.rem(picks, 16) == 15, 1.0, 0.0).astype(BF16)
    pick14 = jnp.where(lax.rem(picks, 16) == 14, 1.0, 0.0).astype(BF16)
    lane = lax.broadcasted_iota(jnp.int32, (TOK, 128), 1)
    low_half = lane < HD
    first = lax.rem(lane, HD) < HD // 2

    def att_weight(start, size):
        return w_att[:, :, :, :, pl.ds(start, size)].reshape(DP, size)

    def swap(tile):
        return jnp.where(first, pltpu.roll(tile, 96, 1), pltpu.roll(tile, 32, 1))

    def gain_rows():
        ga = dot(pick15, att_weight(0, D)).astype(BF16)
        ga = dot(ga, pad_s[...])
        gm = dot(pick14, att_weight(QKV, DP))
        return ga[0:1], gm[0:1]

    def stack(tile_of, kv, ref):
        for j in range(7):
            head = kv * 7 + j
            keep = low_half if head % 2 == 0 else ~low_half
            ref[kv, pl.ds(j * 128, 128), :] = jnp.where(keep, tile_of(head // 2), 0.0).astype(BF16)

    stream = xin[...].astype(F32)
    inv1 = lax.rsqrt(jnp.sum(stream * stream, axis=1, keepdims=True) * (1.0 / D) + eps_norm)
    gain_a, gain_m = gain_rows()
    unit1 = stream * inv1
    u1[...] = unit1
    h1[...] = jnp.where(slot == 14, 1.0, unit1 * gain_a).astype(BF16)

    def project(i):
        cols = span(i * 384, 384, 128)
        proj[:, cols] = dot(h1[...], w_att[:, :, :, :, cols].reshape(DP, 384))

    times(3, project)

    def rotated(j):
        tile = proj[:, pl.ds(128 * j, 128)]
        return tile * cos_t[...] + swap(tile) * sin_t[...]

    def both(tile):
        rolled = pltpu.roll(tile, HD, 1)
        return (
            jnp.where(low_half, tile, rolled).astype(BF16),
            jnp.where(low_half, rolled, tile).astype(BF16),
        )

    for kv in range(KVH):
        stack(rotated, kv, qs)
    kd[0], kd[1] = both(rotated(7))
    vd[0], vd[1] = both(proj[:, pl.ds(1024, 128)])
    allowed = mask[...] > 0.5

    for kv in range(KVH):

        def attend(j, kv=kv):
            rows = span(j * 128, 128, 128)
            s = dot_back(qs[kv, rows, :], kd[kv]) * HD ** (-0.5)
            s = jnp.where(allowed, s, -1e30)
            weights = jnp.exp(s - jnp.max(s, axis=1, keepdims=True))
            probs[kv, rows, :] = weights / jnp.sum(weights, axis=1, keepdims=True)

        times(7, attend)

    def head_out(head):
        kv, j = divmod(head, 7)
        return dot(probs[kv, pl.ds(j * 128, 128), :].astype(BF16), vd[kv])

    mixed = [jnp.where(low_half, head_out(2 * t), head_out(2 * t + 1)).astype(BF16) for t in range(7)]
    obuf[...] = dot(jnp.concatenate(mixed, axis=1), pad_s[...]).astype(BF16)

    def out_project(i):
        cols = span(i * 256, 256, 256)
        x1[:, cols] = xin[:, cols].astype(F32) + dot(
            obuf[...], w_att[:, :, :, :, span(QKV + i * 256, 256, 128)].reshape(DP, 256))

    times(4, out_project)
    middle = x1[...]
    inv2 = lax.rsqrt(jnp.sum(middle * middle, axis=1, keepdims=True) * (1.0 / D) + eps_norm)
    unit2 = middle * inv2
    u2[...] = unit2
    h2all[y] = (unit2 * gain_m).astype(BF16)

    def act_add(part, r):
        def add(c, half, got):
            cols = pl.ds(512 * half, 512)
            part[c, :, cols] = (part[c, :, cols].astype(F32) + got[...].astype(F32)).astype(BF16)

        return add

    def act_gather(ref):
        return Gather(
            lambda c: ref.at[c],
            lambda c: ref.at[c, :, pl.ds(0, 512)],
            lambda c: ref.at[c, :, pl.ds(512, 512)], y, at_y)

    def act_reduce(part, r1, r2):
        return Reduce(
            lambda c: part.at[c],
            lambda c: part.at[c, :, pl.ds(0, 512)],
            lambda c: part.at[c, :, pl.ds(512, 512)], y, at_y, r1, r2, act_add(part, r1))

    def mlp_chunk(c):
        def hidden(i):
            cols = span(i * 256, 256, 256)
            cols_up = span(FP + i * 256, 256, 256)
            gate = dot(h2all[c], w_gu[:, cols])
            upward = dot(h2all[c], w_gu[:, cols_up])
            gact[c, :, cols] = gate
            gact[c, :, cols_up] = upward
            aact[c, :, cols] = (gate * jax.nn.sigmoid(gate) * upward).astype(BF16)

        times(5, hidden)

        def down(i):
            cols = span(i * 256, 256, 256)
            part_f[c, :, cols] = dot(aact[c], w_d[:, cols]).astype(BF16)

        times(4, down)

    ag = act_gather(h2all)
    ag.start()
    mlp_chunk(y)
    ag.mid()
    mlp_chunk(up1(y))
    mlp_chunk(up3(y))
    ag.end()
    mlp_chunk(up2(y))
    rs = act_reduce(part_f, af1, af2)
    rs.start()
    rs.mid()
    rs.end()
    out = x1[...] + (part_f[y].astype(F32) + af2[0].astype(F32) + af2[1].astype(F32))
    ybuf[...] = out.astype(BF16)

    @pl.when(sec == 0)
    def _():
        send_y.start()

    states[...] = dot_back(ybuf[...], pad_s[...]).astype(BF16)

    @pl.when(sec == 0)
    def _():
        send_dx.wait_recv()

    dmall[y] = dyin[...]

    def back_chunk(c):
        def hidden(i):
            cols = span(i * 256, 256, 256)
            cols_up = span(FP + i * 256, 256, 256)
            da = dot_back(dmall[c], w_d[cols, :])
            gate = gact[c, :, cols]
            sig = jax.nn.sigmoid(gate)
            dgu[c, :, cols] = (
                da * gact[c, :, cols_up] * (sig * (1.0 + gate * (1.0 - sig)))).astype(BF16)
            dgu[c, :, cols_up] = (da * gate * sig).astype(BF16)

        times(5, hidden)

        def back(i):
            cols = span(i * 256, 256, 256)
            part_b[c, :, cols] = dot_back(dgu[c], w_gu[cols, :]).astype(BF16)

        times(4, back)

    ag = act_gather(dmall)
    ag.start()
    back_chunk(y)
    ag.mid()
    back_chunk(up1(y))
    back_chunk(up3(y))
    ag.end()
    back_chunk(up2(y))
    rs = act_reduce(part_b, ab1, ab2)
    rs.start()

    g_gu, g_d = w_gu, w_d
    for cp in pending:
        cp.wait_send()
    pending.clear()
    for c in range(RING):
        cols = pl.ds(128 * c, 128)
        h2t[:, cols] = h2all[c].T
        at[:, cols] = aact[c].T
    rs.mid()

    def grad_gu(i):
        cols = span(lax.rem(i, 10) * 256, 256, 256)
        rows = span((i // 10) * 256, 256, 256)
        g_gu[rows, cols] = dot(h2t[rows, :], dgu[:, :, cols].reshape(512, 256)).astype(BF16)

    times(40, grad_gu)

    gu_rows = lambda c: span(256 * c, 256, 256)
    gu_rows_x = lambda c: span(256 * z + 64 * c, 64, 64)
    d_rows_x = lambda c: span(320 * c, 320, 64)
    d_rows_z = lambda c: span(320 * x + 80 * c, 80, 16)

    def flat_add(ref, rows_of, n, width, unit):
        def add(c, half, got):
            cols = pl.ds(width * half, width)
            base = rows_of(c).start

            def step(i):
                there = span(base + unit * i, unit, 16)
                here = span(unit * i, unit, 16)
                ref[there, cols] = (
                    ref[there, cols].astype(F32) + got[here, :].astype(F32)).astype(BF16)

            times(n // unit, step)

        return add

    def flat_total(ref, rows_of, c, n, r2, unit):
        base = rows_of(c).start

        def step(i):
            there = span(base + unit * i, unit, 16)
            here = span(unit * i, unit, 16)
            ref[there, :] = (
                ref[there, :].astype(F32) + r2[0, here, :].astype(F32) + r2[1, here, :].astype(F32)
            ).astype(BF16)

        times(n // unit, step)

    def flat_reduce(ref, rows_of, n, width, c, dev, r1, r2, unit):
        return Reduce(
            lambda k: ref.at[rows_of(k)],
            lambda k: ref.at[rows_of(k), pl.ds(0, width)],
            lambda k: ref.at[rows_of(k), pl.ds(width, width)],
            c, dev, r1, r2, flat_add(ref, rows_of, n, width, unit))

    rgu_z = flat_reduce(g_gu, gu_rows, 256, FP, z, at_z, zg1, zg2, 32)
    rgu_x = flat_reduce(g_gu, gu_rows_x, 64, FP, x, at_x, xg1, xg2, 32)
    rd_x = flat_reduce(g_d, d_rows_x, 320, 512, x, at_x, xd1, xd2, 64)
    rd_z = flat_reduce(g_d, d_rows_z, 80, 512, z, at_z, zd1, zd2, 16)
    rgu_z.start()

    def grad_d(i):
        cols = span(lax.rem(i, 4) * 256, 256, 256)
        rows = span((i // 4) * 256, 256, 256)
        g_d[rows, cols] = dot(at[rows, :], dmall[:, :, cols].reshape(512, 256)).astype(BF16)

    times(20, grad_d)
    rd_x.start()

    rs.end()
    dh2 = part_b[y].astype(F32) + ab2[0].astype(F32) + ab2[1].astype(F32)
    unit2 = u2[...]
    dgain_m = jnp.sum(dh2 * unit2, axis=0, keepdims=True)
    gu2 = dh2 * gain_m
    dx1 = dyin[...].astype(F32) + inv2 * (
        gu2 - unit2 * (jnp.sum(gu2 * unit2, axis=1, keepdims=True) * (1.0 / D)))
    x1[...] = dx1
    datt[...] = dx1.astype(BF16)

    def back_out(i):
        w = w_att[i, :, :, :, pl.ds(QKV, DP)].reshape(256, DP)
        do_buf[:, span(i * 256, 256, 256)] = dot_back(datt[...], w).astype(BF16)

    times(4, back_out)
    rgu_z.mid()
    do_c = dot_back(do_buf[...], pad_s[...])
    do_tile = lambda j: do_c[:, 128 * j : 128 * (j + 1)]
    dq_heads = [None] * QH
    dk_sum = []
    dv_sum = []
    for kv in range(KVH):
        dk = jnp.zeros((TOK, 128), F32)
        dv = jnp.zeros((TOK, 128), F32)
        for j in range(7):
            head = kv * 7 + j
            keep = low_half if head % 2 == 0 else ~low_half
            do_h = jnp.where(keep, do_tile(head // 2), 0.0).astype(BF16)
            pr = probs[kv, pl.ds(j * 128, 128), :]
            dpr = dot_back(do_h, vd[kv])
            ds = (pr * (dpr - jnp.sum(dpr * pr, axis=1, keepdims=True))).astype(BF16)
            dv = dv + dot_rows(pr.astype(BF16), do_h)
            dk = dk + dot_rows(ds, qs[kv, pl.ds(j * 128, 128), :])
            dq_heads[head] = dot(ds, kd[kv]) * HD ** (-0.5)
        dk_sum.append((dk + pltpu.roll(dk, HD, 1)) * HD ** (-0.5))
        dv_sum.append(dv + pltpu.roll(dv, HD, 1))

    def unrotated(tile):
        return (tile * cos_t[...] - swap(tile) * sin_t[...]).astype(BF16)

    for j in range(7):
        dp_buf[:, pl.ds(128 * j, 128)] = unrotated(
            jnp.where(low_half, dq_heads[2 * j], dq_heads[2 * j + 1]))
    dp_buf[:, pl.ds(896, 128)] = unrotated(jnp.where(low_half, dk_sum[0], dk_sum[1]))
    dp_buf[:, pl.ds(1024, 128)] = jnp.where(low_half, dv_sum[0], dv_sum[1]).astype(BF16)

    def back_proj(i):
        w = w_att[i, :, :, :, pl.ds(0, QKV)].reshape(256, QKV)
        dh[:, span(i * 256, 256, 256)] = dot_back(dp_buf[...], w)

    times(4, back_proj)
    dh1 = jnp.where(slot < 14, dh[...], 0.0)
    unit1 = u1[...]
    dgain_a = jnp.sum(dh1 * unit1, axis=0, keepdims=True)
    gu1 = dh1 * gain_a
    dx = x1[...] + inv1 * (
        gu1 - unit1 * (jnp.sum(gu1 * unit1, axis=1, keepdims=True) * (1.0 / D)))
    dx_hi = dx.astype(BF16)
    dxbuf[...] = dx_hi

    @pl.when(sec == 1)
    def _():
        send_dx.start()
        igrads[...] = dot_back(dx_hi, pad_s[...])

    @pl.when(sec == 0)
    def _():
        dx_lo = (dx - dx_hi.astype(F32)).astype(BF16)
        igrads[...] = dot_back(dx_hi, pad_s[...]) + dot_back(dx_lo, pad_s[...])

    h1t = h1[...].T
    ot = obuf[...].T
    proj[0:1, 0:DP] = dgain_a
    dh[0:1, :] = dgain_m
    h2t[:, 0:128] = h1t
    h2t[:, 128:256] = ot
    row = lax.rem(lax.broadcasted_iota(jnp.int32, (256, 256), 0), 16)
    row15 = row == 15
    row14 = row == 14

    def grad_qkv(i):
        zz, n = i // 4, lax.rem(i, 4)
        cols = span(n * 256, 256, 256)
        g = dot(h2t[span(zz * 256, 256, 256), 0:128], dp_buf[:, cols])
        g = jnp.where(row15, proj[0:1, cols], g)
        g_att[zz, :, :, :, cols] = g.astype(BF16).reshape(4, 4, 16, 256)
        g = dot(h2t[span(zz * 256, 256, 256), 128:256], datt[:, cols])
        g = jnp.where(row14, dh[0:1, cols], g)
        g_att[zz, :, :, :, span(QKV + n * 256, 256, 128)] = g.astype(BF16).reshape(4, 4, 16, 256)

    times(16, grad_qkv)

    def grad_v(zz):
        g = dot(h2t[span(zz * 256, 256, 256), 0:128], dp_buf[:, pl.ds(1024, 128)])
        g_att[zz, :, :, :, pl.ds(1024, 128)] = g.astype(BF16).reshape(4, 4, 16, 128)

    times(4, grad_v)

    half_cols = (pl.ds(0, QKV), pl.ds(QKV, DP))

    def add_y(c, half, got):
        cols = half_cols[half]
        size = cols.size

        def step(i):
            a, b = i // 4, lax.rem(i, 4)
            g_att[a, b, c, :, cols] = (
                g_att[a, b, c, :, cols].astype(F32) + got[a, b, :, pl.ds(0, size)].astype(F32)
            ).astype(BF16)

        times(16, step)

    def add_x(c, half, got):
        cols = half_cols[half]
        size = cols.size

        def step(a):
            g_att[a, c, y, :, cols] = (
                g_att[a, c, y, :, cols].astype(F32) + got[a, :, pl.ds(0, size)].astype(F32)
            ).astype(BF16)

        times(4, step)

    def add_z(c, half, got):
        cols = half_cols[half]
        size = cols.size
        g_att[c, x, y, :, cols] = (
            g_att[c, x, y, :, cols].astype(F32) + got[:, pl.ds(0, size)].astype(F32)
        ).astype(BF16)

    class AttReduce(Reduce):
        def start(self):
            c = self.c
            lead = (slice(None),) * self.lead
            low = self.r1.at[(0,) + lead]
            high = self.r1.at[(1,) + lead + (pl.ds(0, DP),)]
            self.a = go(self.low(up2(c)), low, self.dev(up1(c)))
            self.b = go(self.high(up2(c)), high, self.dev(up3(c)))

    def att_reduce(lead, blk, c, dev, r1, r2, add):
        red = AttReduce(
            lambda k: g_att.at[blk(k)],
            lambda k: g_att.at[blk(k) + (slice(None), half_cols[0])],
            lambda k: g_att.at[blk(k) + (slice(None), half_cols[1])],
            c, dev, r1, r2, add)
        red.lead = lead
        return red

    ra_y = att_reduce(3, lambda k: (slice(None), slice(None), k), y, at_y, ya1, ya2, add_y)
    ra_x = att_reduce(2, lambda k: (slice(None), k, y), x, at_x, xa1, xa2, add_x)
    ra_z = att_reduce(1, lambda k: (k, x, y), z, at_z, za1, za2, add_z)
    ra_y.start()
    rd_x.mid()
    ra_y.mid()
    rd_x.end()
    flat_total(g_d, d_rows_x, x, 320, xd2, 64)
    rd_z.start()
    rgu_z.end()
    flat_total(g_gu, gu_rows, z, 256, zg2, 16)
    rgu_x.start()
    ra_y.end()

    def total_y(i):
        a, b = i // 4, lax.rem(i, 4)
        g_att[a, b, y] = (
            g_att[a, b, y].astype(F32) + ya2[0, a, b].astype(F32) + ya2[1, a, b].astype(F32)
        ).astype(BF16)

    times(16, total_y)
    ra_x.start()
    rd_z.mid()
    rgu_x.mid()
    ra_x.mid()
    rd_z.end()
    here = d_rows_z(z)
    tot = g_d[here, :].astype(F32) + zd2[0].astype(F32) + zd2[1].astype(F32)
    hi = tot.astype(BF16)
    lo = (tot - hi.astype(F32)).astype(BF16)
    od[...] = dot_back(hi, pad_s[...]) + dot_back(lo, pad_s[...])
    rgu_x.end()
    flat_total(g_gu, gu_rows_x, x, 64, xg2, 16)
    last = []
    block = lambda c: span(256 * z + 64 * x + 16 * c, 16, 16)
    for step in (up1, up3, up2):
        last.append(go(g_gu.at[block(step(y))], yg.at[y], at_y(step(y))))
    ra_x.end()

    def total_x(a):
        g_att[a, x, y] = (
            g_att[a, x, y].astype(F32) + xa2[0, a].astype(F32) + xa2[1, a].astype(F32)
        ).astype(BF16)

    times(4, total_x)
    ra_z.start()
    ra_z.mid()
    ogu[y] = g_gu[block(y), :]
    for cp in last:
        cp.wait_recv()
    for step in (up1, up3, up2):
        ogu[step(y)] = yg[step(y)]
    ra_z.end()
    tot = g_att[z, x, y].astype(F32) + za2[0].astype(F32) + za2[1].astype(F32)
    oqkv[...] = tot[:, :QKV]
    tot = tot[:, QKV:]
    hi = tot.astype(BF16)
    lo = (tot - hi.astype(F32)).astype(BF16)
    oout[...] = dot_back(hi, pad_s[...]) + dot_back(lo, pad_s[...])

    for cp in pending:
        cp.wait_send()

    @pl.when(sec == 0)
    def _():
        send_y.wait_send()

    @pl.when(sec == 1)
    def _():
        send_dx.wait_send()


def pad_matrix():
    column = np.arange(DP)
    row = np.where(column % 16 < 14, 14 * (column // 16) + column % 16, -1)
    return (np.arange(D)[:, None] == row[None, :]).astype(jnp.bfloat16)


def tables(segments):
    seg = segments.reshape(TOK // ROWS, ROWS)
    earlier = jnp.sum((seg[:, None, :] < seg[:, :, None]).astype(jnp.int32), axis=2)
    place = (jnp.arange(ROWS, dtype=jnp.int32)[None] - earlier).astype(F32).reshape(TOK)
    half = HD // 2
    inverse = theta_base ** (-(jnp.arange(half, dtype=F32) * 2.0 / HD))
    angles = place[:, None] * jnp.tile(inverse, 4)[None, :]
    sign = jnp.where(jnp.arange(128) % HD < half, -1.0, 1.0).astype(F32)
    index = jnp.arange(TOK)
    allowed = (
        (segments[:, None] == segments[None, :])
        & (index[None, :] <= index[:, None])
        & (index[None, :] // ROWS == index[:, None] // ROWS)
    )
    return jnp.cos(angles), jnp.sin(angles) * sign, allowed.astype(F32)


def by_rank(weight):
    pieces = weight.reshape(14, 4, 4, 4, 76).transpose(3, 0, 2, 1, 4)
    return jnp.pad(pieces, ((0, 0), (0, 2), (0, 0), (0, 0), (0, 4))).reshape(4, 16, FP)


def from_rank(grad):
    pieces = grad.reshape(4, 16, 4, 4, 80)[:, :14, :, :, :76]
    return pieces.transpose(1, 3, 2, 0, 4).reshape(1, 14, FF).astype(F32)


def own_row(values, width):
    me = lax.axis_index("fsdp")
    lane = jnp.arange(width)
    n = values.shape[0]
    return jnp.where(lane // n == me, jnp.tile(values, width // n), 0).astype(BF16)[None]


def body(
    tokens, segments, cotangent, w_qkv, b_qkv, w_out, gain_attn, gain_mlp, w_gate, w_up, w_down
):
    me = lax.axis_index("fsdp")
    cos_t, sin_t, mask = tables(segments)
    gu_in = jnp.concatenate([by_rank(w_gate[0]), by_rank(w_up[0])], axis=2)
    d_in = jnp.pad(w_down[0], ((0, 4), (0, 0)))
    gain_row = jnp.pad(own_row(gain_attn[0], D), ((0, 0), (0, QKV - D)))
    qkv_in = jnp.concatenate([w_qkv[0], own_row(b_qkv[0], QKV), gain_row], axis=0)
    out_in = jnp.concatenate([w_out[0], own_row(gain_mlp[0], D), jnp.zeros((1, D), BF16)], axis=0)
    sds = jax.ShapeDtypeStruct
    vm = pltpu.VMEM
    states, igrads, ogu, od, oqkv, oout = pl.pallas_call(
        kernel,
        out_shape=(
            sds((TOK, D), BF16), sds((TOK, D), F32), sds((4, 16, 2 * FP), BF16),
            sds((80, D), F32), sds((16, QKV), F32), sds((16, D), F32),
        ),
        in_specs=[pl.BlockSpec(memory_space=pltpu.VMEM)] * 10,
        out_specs=tuple([pl.BlockSpec(memory_space=pltpu.VMEM)] * 6),
        scratch_shapes=[
            vm((4, 4, 4, 16, ATT), BF16), vm((DP, 2 * FP), BF16), vm((FP, DP), BF16),
            vm((4, 4, 4, 16, ATT), BF16),
            *[vm((TOK, DP), BF16)] * 8, vm((TOK, QKV), BF16),
            vm((4, TOK, DP), BF16), vm((4, TOK, DP), BF16), vm((4, TOK, 2 * FP), F32),
            vm((4, TOK, FP), BF16), vm((4, TOK, 2 * FP), BF16), vm((DP, 512), BF16), vm((FP, 512), BF16),
            vm((4, TOK, DP), BF16), vm((4, TOK, DP), BF16),
            vm((2, TOK, 512), BF16), vm((2, TOK, DP), BF16),
            vm((2, TOK, 512), BF16), vm((2, TOK, DP), BF16), vm((TOK, DP), F32),
            vm((TOK, DP), F32), vm((TOK, DP), F32), vm((TOK, DP), F32), vm((TOK, QKV), F32),
            vm((2, 7 * TOK, 128), BF16), vm((2, TOK, 128), BF16), vm((2, TOK, 128), BF16),
            vm((2, 7 * TOK, 128), F32),
            vm((2, 256, FP), BF16), vm((2, 256, 2 * FP), BF16),
            vm((2, 64, FP), BF16), vm((2, 64, 2 * FP), BF16), vm((4, 16, 2 * FP), BF16),
            vm((2, 320, 512), BF16), vm((2, 320, DP), BF16),
            vm((2, 80, 512), BF16), vm((2, 80, DP), BF16),
            vm((2, 4, 4, 16, QKV), BF16), vm((2, 4, 4, 16, ATT), BF16),
            vm((2, 4, 16, QKV), BF16), vm((2, 4, 16, ATT), BF16),
            vm((2, 16, QKV), BF16), vm((2, 16, ATT), BF16),
            pltpu.SemaphoreType.DMA((N_SEM,)), pltpu.SemaphoreType.DMA((N_SEM,)),
        ],
        compiler_params=pltpu.CompilerParams(
            collective_id=0, has_side_effects=True, vmem_limit_bytes=60 * 2**20
        ),
        cost_estimate=pl.CostEstimate(
            flops=15 * 10**9, bytes_accessed=10 * 2**20, transcendentals=2 * 10**6
        ),
    )(tokens, cotangent, cos_t, sin_t, mask, gu_in, d_in, qkv_in, out_in, jnp.asarray(pad_matrix()))
    gate_grad = from_rank(ogu[:, :, :FP])
    up_grad = from_rank(ogu[:, :, FP:])
    b_grad = lax.dynamic_slice(oqkv, (14, 18 * me), (1, 18))
    ga_grad = lax.dynamic_slice(oqkv, (15, 16 * me), (1, 14))
    gm_grad = lax.dynamic_slice(oout, (14, 14 * me), (1, 14))
    return (
        states[None], igrads[None], oqkv[None, :14], b_grad, oout[None, :14], ga_grad, gm_grad,
        gate_grad, up_grad, od[None, :76],
    )


def solution(mesh):
    return jax.shard_map(
        body,
        mesh=mesh,
        in_specs=(
            P("fsdp", None),
            P("fsdp"),
            P("fsdp", None),
            P("section", "fsdp", None),
            P("section", "fsdp"),
            P("section", "fsdp", None),
            P("section", "fsdp"),
            P("section", "fsdp"),
            P("section", "fsdp", None),
            P("section", "fsdp", None),
            P("section", "fsdp", None),
        ),
        out_specs=(
            P("section", "fsdp", None),
            P("section", "fsdp", None),
            P("section", "fsdp", None),
            P("section", "fsdp"),
            P("section", "fsdp", None),
            P("section", "fsdp"),
            P("section", "fsdp"),
            P("section", "fsdp", None),
            P("section", "fsdp", None),
            P("section", "fsdp", None),
        ),
        check_vma=False,
    )
```

```python
import functools

import jax
import jax.numpy as jnp
import numpy as np
from jax import lax
from jax.experimental import pallas as pl
from jax.experimental.pallas import tpu as pltpu
from jax.sharding import PartitionSpec as P

D = 896
QH = 14
KVH = 2
HD = 64
FF = 4864
QKV = 1152
ROWS = 64
TOK = 128
RING = 4

DP = 1024
FP = 1280
ATT = QKV + DP
N_SEM = 160

eps_norm = 1e-06
theta_base = 1000000.0
MESH = pl.DeviceIdType.MESH
F32 = jnp.float32
BF16 = jnp.bfloat16


def dot(left, right):
    return jnp.dot(left, right, preferred_element_type=F32)


def dot_back(left, right):
    return lax.dot_general(left, right, (((1,), (1,)), ((), ())), preferred_element_type=F32)


def dot_rows(left, right):
    return lax.dot_general(left, right, (((0,), (0,)), ((), ())), preferred_element_type=F32)


def times(n, step):
    def run(i, carry):
        step(i)
        return carry

    lax.fori_loop(0, n, run, 0)


def span(start, size, unit):
    return pl.ds(pl.multiple_of(start, unit), size)


def up1(c):
    return lax.rem(c + 1, RING)


def up2(c):
    return lax.rem(c + 2, RING)


def up3(c):
    return lax.rem(c + 3, RING)


WHOLE = slice(None)
BY_AXES = (("z", "x", "y"), ("y", "z", "x"), ("x", "y", "z"))


def first_whole(index, i):
    k = index.index(WHOLE)
    return index[:k] + (i,) + index[k + 1 :]


def kernel(
    tok, cot, cos_t, sin_t, mask, gu_in, d_in, qkv_in, out_in, vec, pad_s,
    states, igrads, ogu, od, oqkv, oout, ob, oga, ogm,
    w_att, w_gu, w_d, g_out, g_qkv,
    xin, dyin, ybuf, dxbuf, h1, obuf, do_buf, datt, dp_buf, h1t, ot,
    h2all, dmall, gact, aact, dgu, h2t, at,
    part_f, part_b, sum_f, sum_b, dh,
    u1, u2, x1, proj, qs, kd, vd, probs, norms,
    gu1, gu2, gu3, gu4, d1, d2, d3, out1, out2, out3, qkv1, qkv2, qkv3,
    send, recv, turn,
):
    sec = lax.axis_index("section")
    me = lax.axis_index("fsdp")
    at_axis = {"z": me // 16, "x": lax.rem(me // 4, 4), "y": lax.rem(me, 4)}
    z, x, y = at_axis["z"], at_axis["x"], at_axis["y"]

    def device(axis, c):
        place = dict(at_axis)
        place[axis] = c
        return (sec, place["z"] * 16 + place["x"] * 4 + place["y"])

    other = (1 - sec, me)
    barrier = pltpu.get_barrier_semaphore()
    partners = [device(axis, step(at_axis[axis])) for axis in "zxy" for step in (up1, up3, up2)]
    partners.append(other)
    for dev in partners:
        pl.semaphore_signal(barrier, inc=1, device_id=dev, device_id_type=MESH)

    count = [0]
    pending = []

    def remote(src, dst, dev):
        k = count[0]
        count[0] += 1
        return pltpu.make_async_remote_copy(
            src_ref=src, dst_ref=dst, send_sem=send.at[k], recv_sem=recv.at[k],
            device_id=dev, device_id_type=MESH,
        )

    late = []

    def go(cp, pool=pending):
        cp.start()
        if not any(cp is seen for seen in pool):
            pool.append(cp)

    class RingGather:
        def __init__(self, ref, index, cols, cut, axis):
            c = at_axis[axis]
            lo, hi = cols
            whole = lambda k: ref.at[index(k) + (WHOLE, pl.ds(lo, hi - lo))]
            left = lambda k: ref.at[index(k) + (WHOLE, pl.ds(lo, cut - lo))]
            right = lambda k: ref.at[index(k) + (WHOLE, pl.ds(cut, hi - cut))]
            up, down = device(axis, up1(c)), device(axis, up3(c))
            self.a = remote(whole(c), whole(c), up)
            self.b = remote(whole(c), whole(c), down)
            self.e = remote(left(up3(c)), left(up3(c)), up)
            self.f = remote(right(up1(c)), right(up1(c)), down)

        def start(self):
            go(self.a)
            go(self.b)

        def mid(self):
            self.a.wait_recv()
            go(self.e)
            self.b.wait_recv()
            go(self.f)

        def end(self):
            self.e.wait_recv()
            self.f.wait_recv()

    class Gather:
        def __init__(self, ref, index, cols, axis):
            c = at_axis[axis]
            block = ref.at[index(c) + (WHOLE, pl.ds(cols[0], cols[1] - cols[0]))]
            self.copies = [remote(block, block, device(axis, step(c))) for step in (up1, up3, up2)]

        def start(self):
            for cp in self.copies:
                go(cp)

        def end(self):
            for cp in self.copies:
                cp.wait_recv()

    class RingReduce:
        def __init__(self, ref, index, cols, axis, r1, r2):
            c = at_axis[axis]
            lo, hi = cols
            cut = (lo + hi) // 2
            self.ref, self.index, self.c, self.r1, self.r2 = ref, index, c, r1, r2
            self.whole = pl.ds(lo, hi - lo)
            self.left, self.right = pl.ds(lo, cut - lo), pl.ds(cut, hi - cut)
            view = lambda k, part: ref.at[index(k) + (WHOLE, part)]
            up, down = device(axis, up1(c)), device(axis, up3(c))
            self.a = remote(view(up2(c), self.left), r1.at[0], up)
            self.b = remote(view(up2(c), self.right), r1.at[1], down)
            self.e = remote(view(up1(c), self.whole), r2.at[0], up)
            self.f = remote(view(up3(c), self.whole), r2.at[1], down)

        def start(self):
            go(self.a)
            go(self.b)

        def add(self, k, cols, slot):
            def step(i):
                here = first_whole(self.index(k), i) + (WHOLE, cols)
                self.ref[here] = (
                    self.ref[here].astype(F32) + self.r1[slot, i].astype(F32)).astype(BF16)

            times(RING, step)

        def mid(self):
            self.a.wait_recv()
            self.add(up1(self.c), self.left, 0)
            go(self.e)
            self.b.wait_recv()
            self.add(up3(self.c), self.right, 1)
            go(self.f)

        def end(self):
            self.e.wait_recv()
            self.f.wait_recv()

            def step(i):
                here = first_whole(self.index(self.c), i) + (WHOLE, self.whole)
                self.ref[here] = (
                    self.ref[here].astype(F32) + self.r2[0, i].astype(F32) + self.r2[1, i].astype(F32)
                ).astype(BF16)

            times(RING, step)

    class Reduce:
        def __init__(self, ref, index, cols, axis, r):
            c = at_axis[axis]
            part = pl.ds(cols[0], cols[1] - cols[0])
            self.ref, self.r, self.here = ref, r, index(c) + (WHOLE, part)
            self.copies = [
                remote(ref.at[index(step(c)) + (WHOLE, part)], r.at[k], device(axis, step(c)))
                for k, step in enumerate((up1, up3, up2))
            ]

        def start(self):
            for cp in self.copies:
                go(cp)

        def total(self):
            for cp in self.copies:
                cp.wait_recv()
            return self.ref[self.here].astype(F32) + (
                self.r[0].astype(F32) + self.r[1].astype(F32) + self.r[2].astype(F32))

        def end(self):
            self.ref[self.here] = self.total().astype(BF16)

    class TokenGather:
        def __init__(self, ref, pool):
            self.pool = pool
            up, down = device("y", up1(y)), device("y", up3(y))
            self.a = remote(ref.at[0], ref.at[1], up)
            self.b = remote(ref.at[0], ref.at[2], down)
            left, right = pl.ds(0, 512), pl.ds(512, 512)
            self.e = remote(ref.at[1, :, left], ref.at[3, :, left], up)
            self.f = remote(ref.at[2, :, right], ref.at[3, :, right], down)

        def start(self):
            go(self.a, self.pool)
            go(self.b, self.pool)

        def mid(self):
            self.a.wait_recv()
            go(self.e, self.pool)
            self.b.wait_recv()
            go(self.f, self.pool)

        def end(self):
            self.e.wait_recv()
            self.f.wait_recv()

    def gathered(order, phase):
        done = order[:phase]
        return lambda c: tuple(
            WHOLE if a in done else c if a == order[phase] else at_axis[a] for a in ("z", "x", "y"))

    def reduced(order, phase):
        done = order[:phase]
        return lambda c: tuple(
            at_axis[a] if a in done else c if a == order[phase] else WHOLE for a in ("z", "x", "y"))

    mine = pl.ds(pl.multiple_of(16 * y, 16), 16)

    to_rank = [
        remote(gu_in.at[step(y)], w_gu.at[z, x, mine], device("y", step(y))) for step in (up1, up3, up2)]
    gate_x = Gather(w_gu, lambda c: (z, c), (0, FP), "x")
    gate_z = RingGather(w_gu, lambda c: (c, WHOLE), (0, FP), FP // 2, "z")
    up_z = Gather(w_gu, lambda c: (c, x), (FP, 2 * FP), "z")
    up_x = RingGather(w_gu, lambda c: (WHOLE, c), (FP, 2 * FP), FP + FP // 2, "x")
    low_x = Gather(w_d, lambda c: (c, z), (0, 512), "x")
    low_z = RingGather(w_d, lambda c: (WHOLE, c), (0, 512), 256, "z")
    high_z = Gather(w_d, lambda c: (x, c), (512, DP), "z")
    high_x = RingGather(w_d, lambda c: (c, WHOLE), (512, DP), 768, "x")
    att_cols = ((0, QKV), (QKV, QKV + 512), (QKV + 512, ATT))
    att_cut = (640, QKV + 256, QKV + 768)
    att_0 = [Gather(w_att, gathered(o, 0), c, o[0]) for o, c in zip(BY_AXES, att_cols)]
    att_1 = [Gather(w_att, gathered(o, 1), c, o[1]) for o, c in zip(BY_AXES, att_cols)]
    att_2 = [
        RingGather(w_att, gathered(o, 2), c, k, o[2]) for o, c, k in zip(BY_AXES, att_cols, att_cut)]

    pl.semaphore_wait(barrier, len(partners))
    for cp in to_rank:
        go(cp)

    w_gu[z, x, mine, :] = gu_in[y]

    def placed(n, width):
        source = lax.broadcasted_iota(jnp.int32, (128, width), 0)
        target = lax.broadcasted_iota(jnp.int32, (128, width), 1)
        return jnp.where((target == source + n * me) & (source < n), 1.0, 0.0).astype(BF16)

    x1[0:76, pl.ds(0, D)] = d_in[...].astype(F32)
    x1[76:80, pl.ds(0, D)] = jnp.zeros((4, D), F32)
    w_d[x, z] = dot(x1[0:80, pl.ds(0, D)].astype(BF16), pad_s[...]).astype(BF16)
    bias = dot(vec[...], placed(18, QKV))
    gains = dot(vec[...], placed(14, D))
    proj[0:14, :] = qkv_in[...].astype(F32)
    proj[14:15, :] = bias[0:1]
    proj[15:16, pl.ds(0, D)] = gains[1:2]
    proj[15:16, pl.ds(D, QKV - D)] = jnp.zeros((1, QKV - D), F32)
    w_att[z, x, y, :, :QKV] = proj[0:16, :].astype(BF16)
    u1[0:14, pl.ds(0, D)] = out_in[...].astype(F32)
    u1[14:15, pl.ds(0, D)] = gains[2:3]
    u1[15:16, pl.ds(0, D)] = jnp.zeros((1, D), F32)
    w_att[z, x, y, :, QKV:] = dot(u1[0:16, pl.ds(0, D)].astype(BF16), pad_s[...]).astype(BF16)

    for g in att_0:
        g.start()
    low_x.start()
    high_z.start()
    for cp in to_rank:
        cp.wait_recv()

    @pl.when(sec == 1)
    def _():
        pl.semaphore_wait(turn, 1)

    gate_x.start()
    up_z.start()
    for g, after in zip(att_0, att_1):
        g.end()
        after.start()
    low_x.end()
    high_z.end()
    for g, after in zip(att_1, att_2):
        g.end()
        after.start()
    gate_x.end()
    gate_z.start()
    up_z.end()
    up_x.start()
    low_z.start()
    high_x.start()
    for g in att_2:
        g.mid()
    gate_z.mid()
    up_x.mid()

    @pl.when(sec == 0)
    def _():
        pl.semaphore_signal(turn, inc=1, device_id=other, device_id_type=MESH)

    att_2[0].end()

    send_y = remote(ybuf, xin, other)
    send_dx = remote(dxbuf, dyin, other)
    dmg = TokenGather(dmall, late)

    @pl.when(sec == 0)
    def _():
        xin[...] = dot(tok[...], pad_s[...]).astype(BF16)

    @pl.when(sec == 1)
    def _():
        dyin[...] = dot(cot[...], pad_s[...]).astype(BF16)
        dmall[0] = dyin[...]
        dmg.start()
        send_y.wait_recv()

    lanes = lax.broadcasted_iota(jnp.int32, (TOK, DP), 1)
    slot = lax.rem(lanes, 16)
    picks = lax.rem(lax.broadcasted_iota(jnp.int32, (8, DP), 1), 16)
    pick15 = jnp.where(picks == 15, 1.0, 0.0).astype(BF16)
    pick14 = jnp.where(picks == 14, 1.0, 0.0).astype(BF16)
    lane = lax.broadcasted_iota(jnp.int32, (TOK, 128), 1)
    low_half = lane < HD
    first = lax.rem(lane, HD) < HD // 2

    def att_weight(start, size):
        return w_att[:, :, :, :, pl.ds(start, size)].reshape(DP, size)

    def swap(tile):
        return jnp.where(first, pltpu.roll(tile, 96, 1), pltpu.roll(tile, 32, 1))

    stream = xin[...].astype(F32)
    inv1 = lax.rsqrt(jnp.sum(stream * stream, axis=1, keepdims=True) * (1.0 / D) + eps_norm)
    norms[0] = inv1
    gains = dot(pick15, att_weight(0, D)).astype(BF16)
    gain_a = dot(gains, pad_s[...])[0:1]
    unit1 = stream * inv1
    u1[...] = unit1
    h1[...] = jnp.where(slot == 14, 1.0, unit1 * gain_a).astype(BF16)
    for i in range(3):
        proj[:, pl.ds(384 * i, 384)] = dot(h1[...], att_weight(384 * i, 384))

    def rotated(j):
        tile = proj[:, pl.ds(128 * j, 128)]
        return tile * cos_t[...] + swap(tile) * sin_t[...]

    def both(tile):
        rolled = pltpu.roll(tile, HD, 1)
        return (
            jnp.where(low_half, tile, rolled).astype(BF16),
            jnp.where(low_half, rolled, tile).astype(BF16),
        )

    def keep(head):
        return low_half if head % 2 == 0 else ~low_half

    kd[0], kd[1] = both(rotated(7))
    vd[0], vd[1] = both(proj[:, pl.ds(1024, 128)])
    allowed = mask[...] > 0.5
    for t in range(7):
        tile = rotated(t)
        outs = []
        for head in (2 * t, 2 * t + 1):
            kv = head // 7
            q = jnp.where(keep(head), tile, 0.0).astype(BF16)
            qs[head] = q
            s = dot_back(q, kd[kv]) * HD ** (-0.5)
            s = jnp.where(allowed, s, -1e30)
            weights = jnp.exp(s - jnp.max(s, axis=1, keepdims=True))
            pr = weights / jnp.sum(weights, axis=1, keepdims=True)
            probs[head] = pr
            outs.append(dot(pr.astype(BF16), vd[kv]))
        dp_buf[:, pl.ds(128 * t, 128)] = jnp.where(low_half, outs[0], outs[1]).astype(BF16)
    obuf[...] = dot(dp_buf[:, pl.ds(0, D)], pad_s[...]).astype(BF16)
    att_2[1].end()
    att_2[2].end()
    gain_m = dot(pick14, att_weight(QKV, DP))[0:1]
    for i in range(4):
        cols = pl.ds(256 * i, 256)
        x1[:, cols] = xin[:, cols].astype(F32) + dot(obuf[...], att_weight(QKV + 256 * i, 256))
    middle = x1[...]
    inv2 = lax.rsqrt(jnp.sum(middle * middle, axis=1, keepdims=True) * (1.0 / D) + eps_norm)
    norms[1] = inv2
    unit2 = middle * inv2
    u2[...] = unit2
    h2all[0] = (unit2 * gain_m).astype(BF16)

    def token_sums(part, sums):
        return [
            remote(part.at[1], sums.at[0], device("y", up3(y))),
            remote(part.at[2], sums.at[1], device("y", up1(y))),
            remote(part.at[3], sums.at[2], device("y", up2(y))),
        ]

    def token_total(part, sums, copies):
        for cp in copies:
            cp.wait_recv()
        return part[0].astype(F32) + (
            sums[0].astype(F32) + sums[1].astype(F32) + sums[2].astype(F32))

    def mlp(k, n):
        rows = n * TOK
        for i in range(5):
            cols, cols_up = pl.ds(256 * i, 256), pl.ds(FP + 256 * i, 256)
            h = h2all[k : k + n].reshape(rows, DP)
            gate = dot(h, w_gu[:, :, :, cols].reshape(DP, 256))
            upward = dot(h, w_gu[:, :, :, cols_up].reshape(DP, 256))
            gact[k : k + n, :, cols] = gate.reshape(n, TOK, 256)
            gact[k : k + n, :, cols_up] = upward.reshape(n, TOK, 256)
            aact[k : k + n, :, cols] = (
                gate * jax.nn.sigmoid(gate) * upward).astype(BF16).reshape(n, TOK, 256)
        for i in range(4):
            cols = pl.ds(256 * i, 256)
            a = aact[k : k + n].reshape(rows, FP)
            part_f[k : k + n, :, cols] = dot(
                a, w_d[:, :, :, cols].reshape(FP, 256)).astype(BF16).reshape(n, TOK, 256)

    ag = TokenGather(h2all, pending)
    sums = token_sums(part_f, sum_f)
    ag.start()

    @pl.when(sec == 1)
    def _():
        dmg.mid()

    gate_z.end()
    up_x.end()
    low_z.mid()
    high_x.mid()
    low_z.end()
    high_x.end()

    mlp(0, 1)
    ag.mid()
    mlp(1, 2)
    go(sums[0])
    go(sums[1])
    ag.end()
    mlp(3, 1)
    go(sums[2])
    for c in range(RING):
        cols = pl.ds(128 * c, 128)
        h2t[:, cols] = h2all[c].T
        at[:, cols] = aact[c].T
    h1t[...] = h1[...].T
    ot[...] = obuf[...].T
    out = x1[...] + token_total(part_f, sum_f, sums)
    for cp in pending:
        cp.wait_send()
    pending.clear()
    ybuf[...] = out.astype(BF16)

    @pl.when(sec == 0)
    def _():
        send_y.start()


    def store_states():
        states[...] = dot_back(ybuf[...], pad_s[...]).astype(BF16)

    @pl.when(sec == 0)
    def _():
        store_states()
        send_dx.wait_recv()
        dmall[0] = dyin[...]
        dmg.start()

    def mlp_back(k, n):
        rows = n * TOK
        for i in range(2):
            cols, cols_up = pl.ds(640 * i, 640), pl.ds(FP + 640 * i, 640)
            da = dot_back(dmall[k : k + n].reshape(rows, DP), w_d[2 * i : 2 * i + 2].reshape(640, DP))
            gate = gact[k : k + n, :, cols].reshape(rows, 640)
            upward = gact[k : k + n, :, cols_up].reshape(rows, 640)
            sig = jax.nn.sigmoid(gate)
            dgate = da * upward * (sig * (1.0 + gate * (1.0 - sig)))
            dgu[k : k + n, :, cols] = dgate.astype(BF16).reshape(n, TOK, 640)
            dgu[k : k + n, :, cols_up] = (da * gate * sig).astype(BF16).reshape(n, TOK, 640)
        for i in range(4):
            cols = pl.ds(256 * i, 256)
            part_b[k : k + n, :, cols] = dot_back(
                dgu[k : k + n].reshape(rows, 2 * FP), w_gu[i].reshape(256, 2 * FP)
            ).astype(BF16).reshape(n, TOK, 256)

    sums = token_sums(part_b, sum_b)
    mlp_back(0, 1)

    @pl.when(sec == 0)
    def _():
        dmg.mid()

    mlp_back(1, 2)
    go(sums[0])
    go(sums[1])
    dmg.end()
    mlp_back(3, 1)
    go(sums[2])

    rgate_z = RingReduce(w_gu, lambda c: (c, WHOLE), (0, FP), "z", gu1.at[0], gu2.at[0])
    rup_x = RingReduce(w_gu, lambda c: (WHOLE, c), (FP, 2 * FP), "x", gu1.at[1], gu2.at[1])
    rgate_x = Reduce(w_gu, lambda c: (z, c), (0, FP), "x", gu3.at[0])
    rup_z = Reduce(w_gu, lambda c: (c, x), (FP, 2 * FP), "z", gu3.at[1])
    rlow_z = RingReduce(w_d, lambda c: (WHOLE, c), (0, 512), "z", d1.at[0], d2.at[0])
    rhigh_x = RingReduce(w_d, lambda c: (c, WHOLE), (512, DP), "x", d1.at[1], d2.at[1])
    rlow_x = Reduce(w_d, lambda c: (c, z), (0, 512), "x", d3.at[0])
    rhigh_z = Reduce(w_d, lambda c: (x, c), (512, DP), "z", d3.at[1])
    from_rank = [
        remote(
            w_gu.at[z, x, pl.ds(pl.multiple_of(16 * step(y), 16), 16)],
            gu4.at[y], device("y", step(y)))
        for step in (up1, up3, up2)
    ]
    out_red = [
        Reduce(g_out, reduced("yxz", k), (0, DP), "yxz"[k], r) for k, r in enumerate((out1, out2, out3))]
    qkv_order = ("yxz", "xzy", "zyx")
    qkv_red = [
        [
            Reduce(g_qkv, reduced(order, k), (384 * n, 384 * n + 384), order[k], r.at[n])
            for n, order in enumerate(qkv_order)
        ]
        for k, r in enumerate((qkv1, qkv2, qkv3))
    ]

    def gu_terms():
        def grad_gate(i):
            rows = span(256 * i, 256, 256)
            g = dot(h2t[rows, :], dgu[:, :, pl.ds(0, FP)].reshape(512, FP))
            w_gu[i, :, :, pl.ds(0, FP)] = g.astype(BF16).reshape(4, 64, FP)

        def grad_up(i):
            rows = span(256 * i, 256, 256)
            g = dot(h2t[rows, :], dgu[:, :, pl.ds(FP, FP)].reshape(512, FP))
            w_gu[i, :, :, pl.ds(FP, FP)] = g.astype(BF16).reshape(4, 64, FP)

        times(4, grad_gate)
        rgate_z.start()
        times(4, grad_up)
        rup_x.start()

    def d_terms():
        def grad_d(i):
            rows = span(320 * i, 320, 64)
            g = dot(at[rows, :], dmall[...].reshape(512, DP))
            w_d[i] = g.astype(BF16).reshape(4, 80, DP)

        times(4, grad_d)
        rlow_z.start()
        rhigh_x.start()

    row = lax.rem(lax.broadcasted_iota(jnp.int32, (256, 384), 0), 16)

    def out_terms():
        def grad(i):
            g = dot(ot[span(256 * i, 256, 256), :], datt[...])
            g = jnp.where(row14, dh[0:1, :], g)
            g_out[i] = g.astype(BF16).reshape(4, 4, 16, DP)

        row14 = lax.rem(lax.broadcasted_iota(jnp.int32, (256, DP), 0), 16) == 14
        times(4, grad)
        out_red[0].start()

    gu_terms()

    @pl.when(sec == 0)
    def _():
        d_terms()

    dh2 = token_total(part_b, sum_b, sums)
    unit2 = u2[...]
    dh[0:1, :] = jnp.sum(dh2 * unit2, axis=0, keepdims=True)
    gained = dh2 * gain_m
    dx1 = dyin[...].astype(F32) + norms[1] * (
        gained - unit2 * (jnp.sum(gained * unit2, axis=1, keepdims=True) * (1.0 / D)))
    x1[...] = dx1
    datt[...] = dx1.astype(BF16)

    @pl.when(sec == 0)
    def _():
        out_terms()

    for i in range(4):
        w = w_att[i, :, :, :, pl.ds(QKV, DP)].reshape(256, DP)
        do_buf[:, pl.ds(256 * i, 256)] = dot_back(datt[...], w).astype(BF16)
    proj[:, pl.ds(0, D)] = dot_back(do_buf[...], pad_s[...])

    def unrotated(tile):
        return (tile * cos_t[...] - swap(tile) * sin_t[...]).astype(BF16)

    dk_sum = [jnp.zeros((TOK, 128), F32)] * 2
    dv_sum = [jnp.zeros((TOK, 128), F32)] * 2
    for t in range(7):
        tile = proj[:, pl.ds(128 * t, 128)]
        dqs = []
        for head in (2 * t, 2 * t + 1):
            kv = head // 7
            do_h = jnp.where(keep(head), tile, 0.0).astype(BF16)
            pr = probs[head]
            dpr = dot_back(do_h, vd[kv])
            ds = (pr * (dpr - jnp.sum(dpr * pr, axis=1, keepdims=True))).astype(BF16)
            dv_sum[kv] = dv_sum[kv] + dot_rows(pr.astype(BF16), do_h)
            dk_sum[kv] = dk_sum[kv] + dot_rows(ds, qs[head])
            dqs.append(dot(ds, kd[kv]) * HD ** (-0.5))
        dp_buf[:, pl.ds(128 * t, 128)] = unrotated(jnp.where(low_half, dqs[0], dqs[1]))
    dk_sum = [(dk + pltpu.roll(dk, HD, 1)) * HD ** (-0.5) for dk in dk_sum]
    dv_sum = [dv + pltpu.roll(dv, HD, 1) for dv in dv_sum]
    dp_buf[:, pl.ds(896, 128)] = unrotated(jnp.where(low_half, dk_sum[0], dk_sum[1]))
    dp_buf[:, pl.ds(1024, 128)] = jnp.where(low_half, dv_sum[0], dv_sum[1]).astype(BF16)
    rgate_z.mid()
    rup_x.mid()
    for i in range(4):
        w = w_att[i, :, :, :, pl.ds(0, QKV)].reshape(256, QKV)
        proj[:, pl.ds(256 * i, 256)] = dot_back(dp_buf[...], w)
    dh1 = jnp.where(slot < 14, proj[:, pl.ds(0, DP)], 0.0)
    unit1 = u1[...]
    dgain_a = jnp.sum(dh1 * unit1, axis=0, keepdims=True)

    def qkv_terms():
        proj[0:1, pl.ds(0, DP)] = dgain_a
        for n in range(3):
            cols = pl.ds(384 * n, 384)

            def grad(i, cols=cols):
                g = dot(h1t[span(256 * i, 256, 256), :], dp_buf[:, cols])
                g = jnp.where(row == 15, proj[0:1, cols], g)
                g_qkv[i, :, :, :, cols] = g.astype(BF16).reshape(4, 4, 16, 384)

            times(4, grad)
            qkv_red[0][n].start()

    @pl.when(sec == 0)
    def _():
        qkv_terms()

    gained = dh1 * gain_a
    dx = x1[...] + norms[0] * (
        gained - unit1 * (jnp.sum(gained * unit1, axis=1, keepdims=True) * (1.0 / D)))
    dx_hi = dx.astype(BF16)
    dxbuf[...] = dx_hi

    @pl.when(sec == 1)
    def _():
        send_dx.start()
        igrads[...] = dot_back(dx_hi, pad_s[...])
        d_terms()
        out_terms()
        qkv_terms()
        store_states()

    @pl.when(sec == 0)
    def _():
        dx_lo = (dx - dx_hi.astype(F32)).astype(BF16)
        igrads[...] = dot_back(dx_hi, pad_s[...]) + dot_back(dx_lo, pad_s[...])

    rlow_z.mid()
    rhigh_x.mid()
    out_red[0].end()
    out_red[1].start()
    rgate_z.end()
    rgate_x.start()
    rup_x.end()
    rup_z.start()
    for red, after in zip(qkv_red[0], qkv_red[1]):
        red.end()
        after.start()
    rlow_z.end()
    rlow_x.start()
    rhigh_x.end()
    rhigh_z.start()
    out_red[1].end()
    out_red[2].start()
    rgate_x.end()
    rup_z.end()
    for cp in from_rank:
        go(cp)
    for red, after in zip(qkv_red[1], qkv_red[2]):
        red.end()
        after.start()

    def unpadded(total):
        hi = total.astype(BF16)
        lo = (total - hi.astype(F32)).astype(BF16)
        return dot_back(hi, pad_s[...]) + dot_back(lo, pad_s[...])

    def own_lanes(rows, n):
        width = rows.shape[1]
        target = lax.broadcasted_iota(jnp.int32, (width, 128), 1)
        source = lax.broadcasted_iota(jnp.int32, (width, 128), 0)
        move = jnp.where(source == target + n * me, 1.0, 0.0).astype(BF16)
        hi = rows.astype(BF16)
        lo = (rows - hi.astype(F32)).astype(BF16)
        return dot(hi, move) + dot(lo, move)

    od[...] = unpadded(jnp.concatenate([rlow_x.total(), rhigh_z.total()], axis=1))[0:76]
    total = unpadded(out_red[2].total())
    oout[...] = total[0:14]
    ogm[...] = own_lanes(total, 14)[14:15, 0:14]
    for n in range(3):
        proj[0:16, pl.ds(384 * n, 384)] = qkv_red[2][n].total()
    oqkv[...] = proj[0:14, :]
    ob[...] = own_lanes(proj[0:16, :], 18)[14:15, 0:18]
    oga[...] = own_lanes(proj[0:16, pl.ds(0, DP)], 16)[15:16, 0:14]
    ogu[y] = w_gu[z, x, mine, :]
    for cp in from_rank:
        cp.wait_recv()
    for step in (up1, up3, up2):
        ogu[step(y)] = gu4[step(y)]

    for cp in pending + late:
        cp.wait_send()

    @pl.when(sec == 0)
    def _():
        send_y.wait_send()

    @pl.when(sec == 1)
    def _():
        send_dx.wait_send()


def pad_matrix():
    column = np.arange(DP)
    row = np.where(column % 16 < 14, 14 * (column // 16) + column % 16, -1)
    return (np.arange(D)[:, None] == row[None, :]).astype(jnp.bfloat16)


def tables(segments):
    seg = segments.reshape(TOK // ROWS, ROWS)
    earlier = jnp.sum((seg[:, None, :] < seg[:, :, None]).astype(jnp.int32), axis=2)
    place = (jnp.arange(ROWS, dtype=jnp.int32)[None] - earlier).astype(F32).reshape(TOK)
    half = HD // 2
    inverse = theta_base ** (-(jnp.arange(half, dtype=F32) * 2.0 / HD))
    angles = place[:, None] * jnp.tile(inverse, 4)[None, :]
    sign = jnp.where(jnp.arange(128) % HD < half, -1.0, 1.0).astype(F32)
    index = jnp.arange(TOK)
    allowed = (
        (segments[:, None] == segments[None, :])
        & (index[None, :] <= index[:, None])
        & (index[None, :] // ROWS == index[:, None] // ROWS)
    )
    return jnp.cos(angles), jnp.sin(angles) * sign, allowed.astype(F32)


def by_rank(weight):
    pieces = weight.reshape(14, 4, 4, 4, 76).transpose(3, 0, 2, 1, 4)
    return jnp.pad(pieces, ((0, 0), (0, 2), (0, 0), (0, 0), (0, 4))).reshape(4, 16, FP)


def from_rank(grad):
    pieces = grad.reshape(4, 16, 4, 4, 80)[:, :14, :, :, :76]
    return pieces.transpose(1, 3, 2, 0, 4).reshape(1, 14, FF).astype(F32)


def body(
    tokens, segments, cotangent, w_qkv, b_qkv, w_out, gain_attn, gain_mlp, w_gate, w_up, w_down
):
    cos_t, sin_t, mask = tables(segments)
    gu_in = jnp.concatenate([by_rank(w_gate[0]), by_rank(w_up[0])], axis=2)
    vec = jnp.concatenate(
        [jnp.pad(v, ((0, 0), (0, 128 - v.shape[1]))) for v in (b_qkv, gain_attn, gain_mlp)])
    vec = jnp.pad(vec, ((0, 13), (0, 0)))
    sds = jax.ShapeDtypeStruct
    vm = pltpu.VMEM
    states, igrads, ogu, od, oqkv, oout, b_grad, ga_grad, gm_grad = pl.pallas_call(
        kernel,
        out_shape=(
            sds((TOK, D), BF16), sds((TOK, D), F32), sds((4, 16, 2 * FP), BF16),
            sds((76, D), F32), sds((14, QKV), F32), sds((14, D), F32),
            sds((1, 18), F32), sds((1, 14), F32), sds((1, 14), F32),
        ),
        in_specs=[pl.BlockSpec(memory_space=pltpu.VMEM)] * 11,
        out_specs=tuple([pl.BlockSpec(memory_space=pltpu.VMEM)] * 9),
        scratch_shapes=[
            vm((4, 4, 4, 16, ATT), BF16), vm((4, 4, 64, 2 * FP), BF16), vm((4, 4, 80, DP), BF16),
            vm((4, 4, 4, 16, DP), BF16), vm((4, 4, 4, 16, QKV), BF16),
            *[vm((TOK, DP), BF16)] * 8, vm((TOK, QKV), BF16), vm((DP, TOK), BF16), vm((DP, TOK), BF16),
            vm((4, TOK, DP), BF16), vm((4, TOK, DP), BF16), vm((4, TOK, 2 * FP), F32),
            vm((4, TOK, FP), BF16), vm((4, TOK, 2 * FP), BF16), vm((DP, 512), BF16), vm((FP, 512), BF16),
            vm((4, TOK, DP), BF16), vm((4, TOK, DP), BF16),
            vm((3, TOK, DP), BF16), vm((3, TOK, DP), BF16), vm((8, DP), F32),
            vm((TOK, DP), F32), vm((TOK, DP), F32), vm((TOK, DP), F32), vm((TOK, QKV), F32),
            vm((QH, TOK, 128), BF16), vm((2, TOK, 128), BF16), vm((2, TOK, 128), BF16),
            vm((QH, TOK, 128), F32), vm((2, TOK, 1), F32),
            vm((2, 2, 4, 64, FP // 2), BF16), vm((2, 2, 4, 64, FP), BF16),
            vm((2, 3, 64, FP), BF16), vm((4, 16, 2 * FP), BF16),
            vm((2, 2, 4, 80, 256), BF16), vm((2, 2, 4, 80, 512), BF16), vm((2, 3, 80, 512), BF16),
            vm((3, 4, 4, 16, DP), BF16), vm((3, 4, 16, DP), BF16), vm((3, 16, DP), BF16),
            vm((3, 3, 4, 4, 16, 384), BF16), vm((3, 3, 4, 16, 384), BF16), vm((3, 3, 16, 384), BF16),
            pltpu.SemaphoreType.DMA((N_SEM,)), pltpu.SemaphoreType.DMA((N_SEM,)),
            pltpu.SemaphoreType.REGULAR,
        ],
        compiler_params=pltpu.CompilerParams(
            collective_id=0, has_side_effects=True, vmem_limit_bytes=60 * 2**20
        ),
        cost_estimate=pl.CostEstimate(
            flops=15 * 10**9, bytes_accessed=10 * 2**20, transcendentals=2 * 10**6
        ),
    )(
        tokens, cotangent, cos_t, sin_t, mask, gu_in, w_down[0], w_qkv[0], w_out[0], vec,
        jnp.asarray(pad_matrix()),
    )
    return (
        states[None], igrads[None], oqkv[None], b_grad, oout[None], ga_grad, gm_grad,
        from_rank(ogu[:, :, :FP]), from_rank(ogu[:, :, FP:]), od[None],
    )


def solution(mesh):
    return jax.shard_map(
        body,
        mesh=mesh,
        in_specs=(
            P("fsdp", None),
            P("fsdp"),
            P("fsdp", None),
            P("section", "fsdp", None),
            P("section", "fsdp"),
            P("section", "fsdp", None),
            P("section", "fsdp"),
            P("section", "fsdp"),
            P("section", "fsdp", None),
            P("section", "fsdp", None),
            P("section", "fsdp", None),
        ),
        out_specs=(
            P("section", "fsdp", None),
            P("section", "fsdp", None),
            P("section", "fsdp", None),
            P("section", "fsdp"),
            P("section", "fsdp", None),
            P("section", "fsdp"),
            P("section", "fsdp"),
            P("section", "fsdp", None),
            P("section", "fsdp", None),
            P("section", "fsdp", None),
        ),
        check_vma=False,
    )
```

```python
import functools

import jax
import jax.numpy as jnp
import numpy as np
from jax import lax
from jax.experimental import pallas as pl
from jax.experimental.pallas import tpu as pltpu
from jax.sharding import PartitionSpec as P

D = 896
QH = 14
KVH = 2
HD = 64
FF = 4864
QKV = 1152
ROWS = 64
TOK = 128
RING = 4

DP = 1024
FP = 1280
ATT = QKV + DP
N_SEM = 160

eps_norm = 1e-06
theta_base = 1000000.0
MESH = pl.DeviceIdType.MESH
F32 = jnp.float32
BF16 = jnp.bfloat16


def dot(left, right):
    return jnp.dot(left, right, preferred_element_type=F32)


def dot_back(left, right):
    return lax.dot_general(left, right, (((1,), (1,)), ((), ())), preferred_element_type=F32)


def dot_rows(left, right):
    return lax.dot_general(left, right, (((0,), (0,)), ((), ())), preferred_element_type=F32)


def times(n, step):
    def run(i, carry):
        step(i)
        return carry

    lax.fori_loop(0, n, run, 0)


def span(start, size, unit):
    return pl.ds(pl.multiple_of(start, unit), size)


def up1(c):
    return lax.rem(c + 1, RING)


def up2(c):
    return lax.rem(c + 2, RING)


def up3(c):
    return lax.rem(c + 3, RING)


WHOLE = slice(None)
BY_AXES = (("z", "x", "y"), ("y", "z", "x"), ("x", "y", "z"))


def first_whole(index, i):
    k = index.index(WHOLE)
    return index[:k] + (i,) + index[k + 1 :]


def kernel(
    tok, cot, seg, freq, gu_in, d_in, qkv_in, out_in, vec, pad_s,
    states, igrads, ogu, od, oqkv, oout, ob, oga, ogm,
    w_att, w_gu, w_d, g_out, g_qkv,
    xin, dyin, ybuf, dxbuf, h1, obuf, do_buf, datt, dp_buf, h1t, ot,
    h2all, dmall, gact, aact, dgu, h2t, at,
    part_f, part_b, sum_f, sum_b, dh,
    u1, u2, x1, proj, qs, kd, vd, probs, norms,
    gu1, gu2, gu3, gu4, d1, d2, d3, out1, out2, out3, qkv1, qkv2, qkv3,
    cos_t, sin_t, mask, send, recv, turn,
):
    sec = lax.axis_index("section")
    me = lax.axis_index("fsdp")
    at_axis = {"z": me // 16, "x": lax.rem(me // 4, 4), "y": lax.rem(me, 4)}
    z, x, y = at_axis["z"], at_axis["x"], at_axis["y"]

    def device(axis, c):
        place = dict(at_axis)
        place[axis] = c
        return (sec, place["z"] * 16 + place["x"] * 4 + place["y"])

    other = (1 - sec, me)
    barrier = pltpu.get_barrier_semaphore()
    partners = [device(axis, step(at_axis[axis])) for axis in "zxy" for step in (up1, up3, up2)]
    partners.append(other)
    for dev in partners:
        pl.semaphore_signal(barrier, inc=1, device_id=dev, device_id_type=MESH)

    count = [0]
    pending = []

    def remote(src, dst, dev):
        k = count[0]
        count[0] += 1
        return pltpu.make_async_remote_copy(
            src_ref=src, dst_ref=dst, send_sem=send.at[k], recv_sem=recv.at[k],
            device_id=dev, device_id_type=MESH,
        )

    late = []

    def go(cp, pool=pending):
        cp.start()
        if not any(cp is seen for seen in pool):
            pool.append(cp)

    class RingGather:
        def __init__(self, ref, index, cols, cut, axis):
            c = at_axis[axis]
            lo, hi = cols
            whole = lambda k: ref.at[index(k) + (WHOLE, pl.ds(lo, hi - lo))]
            left = lambda k: ref.at[index(k) + (WHOLE, pl.ds(lo, cut - lo))]
            right = lambda k: ref.at[index(k) + (WHOLE, pl.ds(cut, hi - cut))]
            up, down = device(axis, up1(c)), device(axis, up3(c))
            self.a = remote(whole(c), whole(c), up)
            self.b = remote(whole(c), whole(c), down)
            self.e = remote(left(up3(c)), left(up3(c)), up)
            self.f = remote(right(up1(c)), right(up1(c)), down)

        def start(self):
            go(self.a)
            go(self.b)

        def mid(self):
            self.a.wait_recv()
            go(self.e)
            self.b.wait_recv()
            go(self.f)

        def end(self):
            self.e.wait_recv()
            self.f.wait_recv()

    class Gather:
        def __init__(self, ref, index, cols, axis):
            c = at_axis[axis]
            block = ref.at[index(c) + (WHOLE, pl.ds(cols[0], cols[1] - cols[0]))]
            self.copies = [remote(block, block, device(axis, step(c))) for step in (up1, up3, up2)]

        def start(self):
            for cp in self.copies:
                go(cp)

        def end(self):
            for cp in self.copies:
                cp.wait_recv()

    class RingReduce:
        def __init__(self, ref, index, cols, axis, r1, r2):
            c = at_axis[axis]
            lo, hi = cols
            cut = (lo + hi) // 2
            self.ref, self.index, self.c, self.r1, self.r2 = ref, index, c, r1, r2
            self.whole = pl.ds(lo, hi - lo)
            self.left, self.right = pl.ds(lo, cut - lo), pl.ds(cut, hi - cut)
            view = lambda k, part: ref.at[index(k) + (WHOLE, part)]
            up, down = device(axis, up1(c)), device(axis, up3(c))
            self.a = remote(view(up2(c), self.left), r1.at[0], up)
            self.b = remote(view(up2(c), self.right), r1.at[1], down)
            self.e = remote(view(up1(c), self.whole), r2.at[0], up)
            self.f = remote(view(up3(c), self.whole), r2.at[1], down)

        def start(self):
            go(self.a)
            go(self.b)

        def add(self, k, cols, slot):
            def step(i):
                here = first_whole(self.index(k), i) + (WHOLE, cols)
                self.ref[here] = (
                    self.ref[here].astype(F32) + self.r1[slot, i].astype(F32)).astype(BF16)

            times(RING, step)

        def mid(self):
            self.a.wait_recv()
            self.add(up1(self.c), self.left, 0)
            go(self.e)
            self.b.wait_recv()
            self.add(up3(self.c), self.right, 1)
            go(self.f)

        def end(self):
            self.e.wait_recv()
            self.f.wait_recv()

            def step(i):
                here = first_whole(self.index(self.c), i) + (WHOLE, self.whole)
                self.ref[here] = (
                    self.ref[here].astype(F32) + self.r2[0, i].astype(F32) + self.r2[1, i].astype(F32)
                ).astype(BF16)

            times(RING, step)

    class Reduce:
        def __init__(self, ref, index, cols, axis, r):
            c = at_axis[axis]
            part = pl.ds(cols[0], cols[1] - cols[0])
            self.ref, self.r, self.here = ref, r, index(c) + (WHOLE, part)
            self.copies = [
                remote(ref.at[index(step(c)) + (WHOLE, part)], r.at[k], device(axis, step(c)))
                for k, step in enumerate((up1, up3, up2))
            ]

        def start(self):
            for cp in self.copies:
                go(cp)

        def total(self):
            for cp in self.copies:
                cp.wait_recv()
            return self.ref[self.here].astype(F32) + (
                self.r[0].astype(F32) + self.r[1].astype(F32) + self.r[2].astype(F32))

        def end(self):
            self.ref[self.here] = self.total().astype(BF16)

    class TokenGather:
        def __init__(self, ref, pool):
            self.pool = pool
            up, down = device("y", up1(y)), device("y", up3(y))
            self.a = remote(ref.at[0], ref.at[1], up)
            self.b = remote(ref.at[0], ref.at[2], down)
            left, right = pl.ds(0, 512), pl.ds(512, 512)
            self.e = remote(ref.at[1, :, left], ref.at[3, :, left], up)
            self.f = remote(ref.at[2, :, right], ref.at[3, :, right], down)

        def start(self):
            go(self.a, self.pool)
            go(self.b, self.pool)

        def mid(self):
            self.a.wait_recv()
            go(self.e, self.pool)
            self.b.wait_recv()
            go(self.f, self.pool)

        def end(self):
            self.e.wait_recv()
            self.f.wait_recv()

    def gathered(order, phase):
        done = order[:phase]
        return lambda c: tuple(
            WHOLE if a in done else c if a == order[phase] else at_axis[a] for a in ("z", "x", "y"))

    def reduced(order, phase):
        done = order[:phase]
        return lambda c: tuple(
            at_axis[a] if a in done else c if a == order[phase] else WHOLE for a in ("z", "x", "y"))

    mine = pl.ds(pl.multiple_of(16 * y, 16), 16)

    to_rank = [
        remote(gu_in.at[step(y)], w_gu.at[z, x, mine], device("y", step(y))) for step in (up1, up3, up2)]
    gate_x = Gather(w_gu, lambda c: (z, c), (0, FP), "x")
    gate_z = RingGather(w_gu, lambda c: (c, WHOLE), (0, FP), FP // 2, "z")
    up_z = Gather(w_gu, lambda c: (c, x), (FP, 2 * FP), "z")
    up_x = RingGather(w_gu, lambda c: (WHOLE, c), (FP, 2 * FP), FP + FP // 2, "x")
    low_x = Gather(w_d, lambda c: (c, z), (0, 512), "x")
    low_z = RingGather(w_d, lambda c: (WHOLE, c), (0, 512), 256, "z")
    high_z = Gather(w_d, lambda c: (x, c), (512, DP), "z")
    high_x = RingGather(w_d, lambda c: (c, WHOLE), (512, DP), 768, "x")
    att_cols = ((0, QKV), (QKV, QKV + 512), (QKV + 512, ATT))
    att_cut = (640, QKV + 256, QKV + 768)
    att_0 = [Gather(w_att, gathered(o, 0), c, o[0]) for o, c in zip(BY_AXES, att_cols)]
    att_1 = [Gather(w_att, gathered(o, 1), c, o[1]) for o, c in zip(BY_AXES, att_cols)]
    att_2 = [
        RingGather(w_att, gathered(o, 2), c, k, o[2]) for o, c, k in zip(BY_AXES, att_cols, att_cut)]

    pl.semaphore_wait(barrier, len(partners))
    for cp in to_rank:
        go(cp)

    w_gu[z, x, mine, :] = gu_in[y]

    def placed(n, width):
        source = lax.broadcasted_iota(jnp.int32, (128, width), 0)
        target = lax.broadcasted_iota(jnp.int32, (128, width), 1)
        return jnp.where((target == source + n * me) & (source < n), 1.0, 0.0).astype(BF16)

    x1[0:76, pl.ds(0, D)] = d_in[...].astype(F32)
    x1[76:80, pl.ds(0, D)] = jnp.zeros((4, D), F32)
    w_d[x, z] = dot(x1[0:80, pl.ds(0, D)].astype(BF16), pad_s[...]).astype(BF16)
    bias = dot(vec[...], placed(18, QKV))
    gains = dot(vec[...], placed(14, D))
    proj[0:14, :] = qkv_in[...].astype(F32)
    proj[14:15, :] = bias[0:1]
    proj[15:16, pl.ds(0, D)] = gains[1:2]
    proj[15:16, pl.ds(D, QKV - D)] = jnp.zeros((1, QKV - D), F32)
    w_att[z, x, y, :, :QKV] = proj[0:16, :].astype(BF16)
    u1[0:14, pl.ds(0, D)] = out_in[...].astype(F32)
    u1[14:15, pl.ds(0, D)] = gains[2:3]
    u1[15:16, pl.ds(0, D)] = jnp.zeros((1, D), F32)
    w_att[z, x, y, :, QKV:] = dot(u1[0:16, pl.ds(0, D)].astype(BF16), pad_s[...]).astype(BF16)

    for g in att_0:
        g.start()
    low_x.start()
    high_z.start()

    for cp in to_rank:
        cp.wait_recv()

    @pl.when(sec == 1)
    def _():
        pl.semaphore_wait(turn, 1)

    gate_x.start()
    up_z.start()

    row_no = lax.broadcasted_iota(jnp.int32, (TOK, TOK), 0)
    col_no = lax.broadcasted_iota(jnp.int32, (TOK, TOK), 1)
    seg_j = jnp.broadcast_to(seg[...].astype(F32), (TOK, TOK))
    seg_i = seg_j.T
    same_block = jnp.where(row_no < ROWS, 0, 1) == jnp.where(col_no < ROWS, 0, 1)
    earlier = jnp.sum(
        jnp.where(same_block & (seg_j < seg_i), 1.0, 0.0), axis=1, keepdims=True)
    place = jnp.where(row_no < ROWS, row_no, row_no - ROWS).astype(F32) - earlier
    angles = place * freq[0:1]
    cos_t[...] = jnp.cos(angles)
    sin_t[...] = jnp.sin(angles) * freq[1:2]
    mask[...] = jnp.where(same_block & (seg_j == seg_i) & (col_no <= row_no), 1.0, 0.0)
    for g, after in zip(att_0, att_1):
        g.end()
        after.start()
    gate_x.end()
    gate_z.start()
    up_z.end()
    up_x.start()
    for g, after in zip(att_1, att_2):
        g.end()
        after.start()
    low_x.end()
    high_z.end()
    low_z.start()
    high_x.start()
    for g in att_2:
        g.mid()
    gate_z.mid()
    up_x.mid()
    low_z.mid()
    high_x.mid()

    @pl.when(sec == 0)
    def _():
        pl.semaphore_signal(turn, inc=1, device_id=other, device_id_type=MESH)

    att_2[0].end()

    send_y = remote(ybuf, xin, other)
    send_dx = remote(dxbuf, dyin, other)
    dmg = TokenGather(dmall, late)

    @pl.when(sec == 0)
    def _():
        xin[...] = dot(tok[...], pad_s[...]).astype(BF16)

    @pl.when(sec == 1)
    def _():
        dyin[...] = dot(cot[...], pad_s[...]).astype(BF16)
        dmall[0] = dyin[...]
        dmg.start()
        send_y.wait_recv()

    lanes = lax.broadcasted_iota(jnp.int32, (TOK, DP), 1)
    slot = lax.rem(lanes, 16)
    picks = lax.rem(lax.broadcasted_iota(jnp.int32, (8, DP), 1), 16)
    pick15 = jnp.where(picks == 15, 1.0, 0.0).astype(BF16)
    pick14 = jnp.where(picks == 14, 1.0, 0.0).astype(BF16)
    lane = lax.broadcasted_iota(jnp.int32, (TOK, 128), 1)
    low_half = lane < HD
    first = lax.rem(lane, HD) < HD // 2

    def att_weight(start, size):
        return w_att[:, :, :, :, pl.ds(start, size)].reshape(DP, size)

    def swap(tile):
        return jnp.where(first, pltpu.roll(tile, 96, 1), pltpu.roll(tile, 32, 1))

    stream = xin[...].astype(F32)
    inv1 = lax.rsqrt(jnp.sum(stream * stream, axis=1, keepdims=True) * (1.0 / D) + eps_norm)
    norms[0] = inv1
    gains = dot(pick15, att_weight(0, D)).astype(BF16)
    gain_a = dot(gains, pad_s[...])[0:1]
    unit1 = stream * inv1
    u1[...] = unit1
    h1[...] = jnp.where(slot == 14, 1.0, unit1 * gain_a).astype(BF16)
    for i in range(3):
        proj[:, pl.ds(384 * i, 384)] = dot(h1[...], att_weight(384 * i, 384))

    def rotated(j):
        tile = proj[:, pl.ds(128 * j, 128)]
        return tile * cos_t[...] + swap(tile) * sin_t[...]

    def both(tile):
        rolled = pltpu.roll(tile, HD, 1)
        return (
            jnp.where(low_half, tile, rolled).astype(BF16),
            jnp.where(low_half, rolled, tile).astype(BF16),
        )

    def keep(head):
        return low_half if head % 2 == 0 else ~low_half

    kd[0], kd[1] = both(rotated(7))
    vd[0], vd[1] = both(proj[:, pl.ds(1024, 128)])
    allowed = mask[...] > 0.5
    for t in range(7):
        tile = rotated(t)
        outs = []
        for head in (2 * t, 2 * t + 1):
            kv = head // 7
            q = jnp.where(keep(head), tile, 0.0).astype(BF16)
            qs[head] = q
            s = dot_back(q, kd[kv]) * HD ** (-0.5)
            s = jnp.where(allowed, s, -1e30)
            weights = jnp.exp(s - jnp.max(s, axis=1, keepdims=True))
            pr = weights / jnp.sum(weights, axis=1, keepdims=True)
            probs[head] = pr
            outs.append(dot(pr.astype(BF16), vd[kv]))
        dp_buf[:, pl.ds(128 * t, 128)] = jnp.where(low_half, outs[0], outs[1]).astype(BF16)
    obuf[...] = dot(dp_buf[:, pl.ds(0, D)], pad_s[...]).astype(BF16)
    att_2[1].end()
    att_2[2].end()
    gain_m = dot(pick14, att_weight(QKV, DP))[0:1]
    for i in range(4):
        cols = pl.ds(256 * i, 256)
        x1[:, cols] = xin[:, cols].astype(F32) + dot(obuf[...], att_weight(QKV + 256 * i, 256))
    middle = x1[...]
    inv2 = lax.rsqrt(jnp.sum(middle * middle, axis=1, keepdims=True) * (1.0 / D) + eps_norm)
    norms[1] = inv2
    unit2 = middle * inv2
    u2[...] = unit2
    h2all[0] = (unit2 * gain_m).astype(BF16)

    def token_sums(part, sums):
        return [
            remote(part.at[1], sums.at[0], device("y", up3(y))),
            remote(part.at[2], sums.at[1], device("y", up1(y))),
            remote(part.at[3], sums.at[2], device("y", up2(y))),
        ]

    def token_total(part, sums, copies):
        for cp in copies:
            cp.wait_recv()
        return part[0].astype(F32) + (
            sums[0].astype(F32) + sums[1].astype(F32) + sums[2].astype(F32))

    def mlp(k, n):
        rows = n * TOK
        for i in range(5):
            cols, cols_up = pl.ds(256 * i, 256), pl.ds(FP + 256 * i, 256)
            h = h2all[k : k + n].reshape(rows, DP)
            gate = dot(h, w_gu[:, :, :, cols].reshape(DP, 256))
            upward = dot(h, w_gu[:, :, :, cols_up].reshape(DP, 256))
            gact[k : k + n, :, cols] = gate.reshape(n, TOK, 256)
            gact[k : k + n, :, cols_up] = upward.reshape(n, TOK, 256)
            aact[k : k + n, :, cols] = (
                gate * jax.nn.sigmoid(gate) * upward).astype(BF16).reshape(n, TOK, 256)
        for i in range(4):
            cols = pl.ds(256 * i, 256)
            a = aact[k : k + n].reshape(rows, FP)
            part_f[k : k + n, :, cols] = dot(
                a, w_d[:, :, :, cols].reshape(FP, 256)).astype(BF16).reshape(n, TOK, 256)

    ag = TokenGather(h2all, pending)
    sums = token_sums(part_f, sum_f)
    ag.start()

    @pl.when(sec == 1)
    def _():
        dmg.mid()

    gate_z.end()
    up_x.end()
    low_z.end()
    high_x.end()

    mlp(0, 1)
    ag.mid()
    mlp(1, 2)
    go(sums[0])
    go(sums[1])
    ag.end()
    mlp(3, 1)
    go(sums[2])
    for c in range(RING):
        cols = pl.ds(128 * c, 128)
        h2t[:, cols] = h2all[c].T
        at[:, cols] = aact[c].T
    h1t[...] = h1[...].T
    ot[...] = obuf[...].T
    out = x1[...] + token_total(part_f, sum_f, sums)
    for cp in pending:
        cp.wait_send()
    pending.clear()
    ybuf[...] = out.astype(BF16)

    @pl.when(sec == 0)
    def _():
        send_y.start()


    def store_states():
        states[...] = dot_back(ybuf[...], pad_s[...]).astype(BF16)

    @pl.when(sec == 0)
    def _():
        store_states()
        send_dx.wait_recv()
        dmall[0] = dyin[...]
        dmg.start()

    def mlp_back(k, n):
        rows = n * TOK
        for i in range(2):
            cols, cols_up = pl.ds(640 * i, 640), pl.ds(FP + 640 * i, 640)
            da = dot_back(dmall[k : k + n].reshape(rows, DP), w_d[2 * i : 2 * i + 2].reshape(640, DP))
            gate = gact[k : k + n, :, cols].reshape(rows, 640)
            upward = gact[k : k + n, :, cols_up].reshape(rows, 640)
            sig = jax.nn.sigmoid(gate)
            dgate = da * upward * (sig * (1.0 + gate * (1.0 - sig)))
            dgu[k : k + n, :, cols] = dgate.astype(BF16).reshape(n, TOK, 640)
            dgu[k : k + n, :, cols_up] = (da * gate * sig).astype(BF16).reshape(n, TOK, 640)
        for i in range(4):
            cols = pl.ds(256 * i, 256)
            part_b[k : k + n, :, cols] = dot_back(
                dgu[k : k + n].reshape(rows, 2 * FP), w_gu[i].reshape(256, 2 * FP)
            ).astype(BF16).reshape(n, TOK, 256)

    sums = token_sums(part_b, sum_b)
    mlp_back(0, 1)

    @pl.when(sec == 0)
    def _():
        dmg.mid()

    mlp_back(1, 2)
    go(sums[0])
    go(sums[1])
    dmg.end()
    mlp_back(3, 1)
    go(sums[2])

    rgate_z = RingReduce(w_gu, lambda c: (c, WHOLE), (0, FP), "z", gu1.at[0], gu2.at[0])
    rup_x = RingReduce(w_gu, lambda c: (WHOLE, c), (FP, 2 * FP), "x", gu1.at[1], gu2.at[1])
    rgate_x = Reduce(w_gu, lambda c: (z, c), (0, FP), "x", gu3.at[0])
    rup_z = Reduce(w_gu, lambda c: (c, x), (FP, 2 * FP), "z", gu3.at[1])
    rlow_z = RingReduce(w_d, lambda c: (WHOLE, c), (0, 512), "z", d1.at[0], d2.at[0])
    rhigh_x = RingReduce(w_d, lambda c: (c, WHOLE), (512, DP), "x", d1.at[1], d2.at[1])
    rlow_x = Reduce(w_d, lambda c: (c, z), (0, 512), "x", d3.at[0])
    rhigh_z = Reduce(w_d, lambda c: (x, c), (512, DP), "z", d3.at[1])
    from_rank = [
        remote(
            w_gu.at[z, x, pl.ds(pl.multiple_of(16 * step(y), 16), 16)],
            gu4.at[y], device("y", step(y)))
        for step in (up1, up3, up2)
    ]
    out_red = [
        Reduce(g_out, reduced("yxz", k), (0, DP), "yxz"[k], r) for k, r in enumerate((out1, out2, out3))]
    qkv_order = ("yxz", "xzy", "zyx")
    qkv_red = [
        [
            Reduce(g_qkv, reduced(order, k), (384 * n, 384 * n + 384), order[k], r.at[n])
            for n, order in enumerate(qkv_order)
        ]
        for k, r in enumerate((qkv1, qkv2, qkv3))
    ]

    def gu_terms():
        def grad_gate(i):
            rows = span(256 * i, 256, 256)
            g = dot(h2t[rows, :], dgu[:, :, pl.ds(0, FP)].reshape(512, FP))
            w_gu[i, :, :, pl.ds(0, FP)] = g.astype(BF16).reshape(4, 64, FP)

        def grad_up(i):
            rows = span(256 * i, 256, 256)
            g = dot(h2t[rows, :], dgu[:, :, pl.ds(FP, FP)].reshape(512, FP))
            w_gu[i, :, :, pl.ds(FP, FP)] = g.astype(BF16).reshape(4, 64, FP)

        times(4, grad_gate)
        rgate_z.start()
        times(4, grad_up)
        rup_x.start()

    def d_terms():
        def grad_d(i):
            rows = span(320 * i, 320, 64)
            g = dot(at[rows, :], dmall[...].reshape(512, DP))
            w_d[i] = g.astype(BF16).reshape(4, 80, DP)

        times(4, grad_d)
        rlow_z.start()
        rhigh_x.start()

    row = lax.rem(lax.broadcasted_iota(jnp.int32, (256, 384), 0), 16)

    def out_terms():
        def grad(i):
            g = dot(ot[span(256 * i, 256, 256), :], datt[...])
            g = jnp.where(row14, dh[0:1, :], g)
            g_out[i] = g.astype(BF16).reshape(4, 4, 16, DP)

        row14 = lax.rem(lax.broadcasted_iota(jnp.int32, (256, DP), 0), 16) == 14
        times(4, grad)
        out_red[0].start()

    gu_terms()

    @pl.when(sec == 0)
    def _():
        d_terms()

    dh2 = token_total(part_b, sum_b, sums)
    unit2 = u2[...]
    dh[0:1, :] = jnp.sum(dh2 * unit2, axis=0, keepdims=True)
    gained = dh2 * gain_m
    dx1 = dyin[...].astype(F32) + norms[1] * (
        gained - unit2 * (jnp.sum(gained * unit2, axis=1, keepdims=True) * (1.0 / D)))
    x1[...] = dx1
    datt[...] = dx1.astype(BF16)

    @pl.when(sec == 0)
    def _():
        out_terms()

    for i in range(4):
        w = w_att[i, :, :, :, pl.ds(QKV, DP)].reshape(256, DP)
        do_buf[:, pl.ds(256 * i, 256)] = dot_back(datt[...], w).astype(BF16)
    proj[:, pl.ds(0, D)] = dot_back(do_buf[...], pad_s[...])

    def unrotated(tile):
        return (tile * cos_t[...] - swap(tile) * sin_t[...]).astype(BF16)

    dk_sum = [jnp.zeros((TOK, 128), F32)] * 2
    dv_sum = [jnp.zeros((TOK, 128), F32)] * 2
    for t in range(7):
        tile = proj[:, pl.ds(128 * t, 128)]
        dqs = []
        for head in (2 * t, 2 * t + 1):
            kv = head // 7
            do_h = jnp.where(keep(head), tile, 0.0).astype(BF16)
            pr = probs[head]
            dpr = dot_back(do_h, vd[kv])
            ds = (pr * (dpr - jnp.sum(dpr * pr, axis=1, keepdims=True))).astype(BF16)
            dv_sum[kv] = dv_sum[kv] + dot_rows(pr.astype(BF16), do_h)
            dk_sum[kv] = dk_sum[kv] + dot_rows(ds, qs[head])
            dqs.append(dot(ds, kd[kv]) * HD ** (-0.5))
        dp_buf[:, pl.ds(128 * t, 128)] = unrotated(jnp.where(low_half, dqs[0], dqs[1]))
    dk_sum = [(dk + pltpu.roll(dk, HD, 1)) * HD ** (-0.5) for dk in dk_sum]
    dv_sum = [dv + pltpu.roll(dv, HD, 1) for dv in dv_sum]
    dp_buf[:, pl.ds(896, 128)] = unrotated(jnp.where(low_half, dk_sum[0], dk_sum[1]))
    dp_buf[:, pl.ds(1024, 128)] = jnp.where(low_half, dv_sum[0], dv_sum[1]).astype(BF16)
    rgate_z.mid()
    rup_x.mid()
    for i in range(4):
        w = w_att[i, :, :, :, pl.ds(0, QKV)].reshape(256, QKV)
        proj[:, pl.ds(256 * i, 256)] = dot_back(dp_buf[...], w)
    dh1 = jnp.where(slot < 14, proj[:, pl.ds(0, DP)], 0.0)
    unit1 = u1[...]
    dgain_a = jnp.sum(dh1 * unit1, axis=0, keepdims=True)

    def qkv_terms():
        proj[0:1, pl.ds(0, DP)] = dgain_a
        for n in range(3):
            cols = pl.ds(384 * n, 384)

            def grad(i, cols=cols):
                g = dot(h1t[span(256 * i, 256, 256), :], dp_buf[:, cols])
                g = jnp.where(row == 15, proj[0:1, cols], g)
                g_qkv[i, :, :, :, cols] = g.astype(BF16).reshape(4, 4, 16, 384)

            times(4, grad)
            qkv_red[0][n].start()

    @pl.when(sec == 0)
    def _():
        qkv_terms()

    gained = dh1 * gain_a
    dx = x1[...] + norms[0] * (
        gained - unit1 * (jnp.sum(gained * unit1, axis=1, keepdims=True) * (1.0 / D)))
    dx_hi = dx.astype(BF16)
    dxbuf[...] = dx_hi

    @pl.when(sec == 1)
    def _():
        send_dx.start()
        igrads[...] = dot_back(dx_hi, pad_s[...])
        d_terms()
        out_terms()
        qkv_terms()
        store_states()

    @pl.when(sec == 0)
    def _():
        dx_lo = (dx - dx_hi.astype(F32)).astype(BF16)
        igrads[...] = dot_back(dx_hi, pad_s[...]) + dot_back(dx_lo, pad_s[...])

    rlow_z.mid()
    rhigh_x.mid()
    out_red[0].end()
    out_red[1].start()
    rgate_z.end()
    rgate_x.start()
    rup_x.end()
    rup_z.start()
    for red, after in zip(qkv_red[0], qkv_red[1]):
        red.end()
        after.start()
    rlow_z.end()
    rlow_x.start()
    rhigh_x.end()
    rhigh_z.start()
    out_red[1].end()
    out_red[2].start()
    rgate_x.end()
    rup_z.end()
    for cp in from_rank:
        go(cp)
    for red, after in zip(qkv_red[1], qkv_red[2]):
        red.end()
        after.start()

    def unpadded(total):
        hi = total.astype(BF16)
        lo = (total - hi.astype(F32)).astype(BF16)
        return dot_back(hi, pad_s[...]) + dot_back(lo, pad_s[...])

    def own_lanes(rows, n):
        width = rows.shape[1]
        target = lax.broadcasted_iota(jnp.int32, (width, 128), 1)
        source = lax.broadcasted_iota(jnp.int32, (width, 128), 0)
        move = jnp.where(source == target + n * me, 1.0, 0.0).astype(BF16)
        hi = rows.astype(BF16)
        lo = (rows - hi.astype(F32)).astype(BF16)
        return dot(hi, move) + dot(lo, move)

    def by_row(ref, rows):
        for r in range(ref.shape[0]):
            ref[r] = rows[r : r + 1]

    by_row(od, unpadded(jnp.concatenate([rlow_x.total(), rhigh_z.total()], axis=1)))
    total = unpadded(out_red[2].total())
    by_row(oout, total)
    ogm[...] = own_lanes(total, 14)[14:15, 0:14]
    for n in range(3):
        proj[0:16, pl.ds(384 * n, 384)] = qkv_red[2][n].total()
    by_row(oqkv, proj[0:16, :])
    ob[...] = own_lanes(proj[0:16, :], 18)[14:15, 0:18]
    oga[...] = own_lanes(proj[0:16, pl.ds(0, DP)], 16)[15:16, 0:14]
    ogu[y] = w_gu[z, x, mine, :]
    for cp in from_rank:
        cp.wait_recv()
    for step in (up1, up3, up2):
        ogu[step(y)] = gu4[step(y)]

    for cp in pending + late:
        cp.wait_send()

    @pl.when(sec == 0)
    def _():
        send_y.wait_send()

    @pl.when(sec == 1)
    def _():
        send_dx.wait_send()


def pad_matrix():
    column = np.arange(DP)
    row = np.where(column % 16 < 14, 14 * (column // 16) + column % 16, -1)
    return (np.arange(D)[:, None] == row[None, :]).astype(jnp.bfloat16)


def frequencies():
    half = HD // 2
    inverse = theta_base ** (-(np.arange(half, dtype=np.float64) * 2.0 / HD))
    sign = np.where(np.arange(128) % HD < half, -1.0, 1.0)
    return np.concatenate([np.tile(inverse, 4)[None], sign[None], np.zeros((6, 128))]).astype(np.float32)


def by_rank(weight):
    pieces = weight.reshape(14, 4, 4, 4, 76).transpose(3, 0, 2, 1, 4)
    return jnp.pad(pieces, ((0, 0), (0, 2), (0, 0), (0, 0), (0, 4))).reshape(4, 16, FP)


def from_rank(grad):
    pieces = grad.reshape(4, 16, 4, 4, 80)[:, :14, :, :, :76]
    return pieces.transpose(1, 3, 2, 0, 4).reshape(1, 14, FF).astype(F32)


def body(
    tokens, segments, cotangent, w_qkv, b_qkv, w_out, gain_attn, gain_mlp, w_gate, w_up, w_down
):
    gu_in = jnp.concatenate([by_rank(w_gate[0]), by_rank(w_up[0])], axis=2)
    vec = jnp.concatenate(
        [jnp.pad(v, ((0, 0), (0, 128 - v.shape[1]))) for v in (b_qkv, gain_attn, gain_mlp)])
    vec = jnp.pad(vec, ((0, 13), (0, 0)))
    sds = jax.ShapeDtypeStruct
    vm = pltpu.VMEM
    states, igrads, ogu, od, oqkv, oout, b_grad, ga_grad, gm_grad = pl.pallas_call(
        kernel,
        out_shape=(
            sds((TOK, D), BF16), sds((TOK, D), F32), sds((4, 16, 2 * FP), BF16),
            sds((76, 1, D), F32), sds((14, 1, QKV), F32), sds((14, 1, D), F32),
            sds((1, 18), F32), sds((1, 14), F32), sds((1, 14), F32),
        ),
        in_specs=[pl.BlockSpec(memory_space=pltpu.VMEM)] * 10,
        out_specs=tuple([pl.BlockSpec(memory_space=pltpu.VMEM)] * 9),
        scratch_shapes=[
            vm((4, 4, 4, 16, ATT), BF16), vm((4, 4, 64, 2 * FP), BF16), vm((4, 4, 80, DP), BF16),
            vm((4, 4, 4, 16, DP), BF16), vm((4, 4, 4, 16, QKV), BF16),
            *[vm((TOK, DP), BF16)] * 8, vm((TOK, QKV), BF16), vm((DP, TOK), BF16), vm((DP, TOK), BF16),
            vm((4, TOK, DP), BF16), vm((4, TOK, DP), BF16), vm((4, TOK, 2 * FP), F32),
            vm((4, TOK, FP), BF16), vm((4, TOK, 2 * FP), BF16), vm((DP, 512), BF16), vm((FP, 512), BF16),
            vm((4, TOK, DP), BF16), vm((4, TOK, DP), BF16),
            vm((3, TOK, DP), BF16), vm((3, TOK, DP), BF16), vm((8, DP), F32),
            vm((TOK, DP), F32), vm((TOK, DP), F32), vm((TOK, DP), F32), vm((TOK, QKV), F32),
            vm((QH, TOK, 128), BF16), vm((2, TOK, 128), BF16), vm((2, TOK, 128), BF16),
            vm((QH, TOK, 128), F32), vm((2, TOK, 1), F32),
            vm((2, 2, 4, 64, FP // 2), BF16), vm((2, 2, 4, 64, FP), BF16),
            vm((2, 3, 64, FP), BF16), vm((4, 16, 2 * FP), BF16),
            vm((2, 2, 4, 80, 256), BF16), vm((2, 2, 4, 80, 512), BF16), vm((2, 3, 80, 512), BF16),
            vm((3, 4, 4, 16, DP), BF16), vm((3, 4, 16, DP), BF16), vm((3, 16, DP), BF16),
            vm((3, 3, 4, 4, 16, 384), BF16), vm((3, 3, 4, 16, 384), BF16), vm((3, 3, 16, 384), BF16),
            *[vm((TOK, TOK), F32)] * 3,
            pltpu.SemaphoreType.DMA((N_SEM,)), pltpu.SemaphoreType.DMA((N_SEM,)),
            pltpu.SemaphoreType.REGULAR,
        ],
        compiler_params=pltpu.CompilerParams(
            collective_id=0, has_side_effects=True, vmem_limit_bytes=60 * 2**20
        ),
        cost_estimate=pl.CostEstimate(
            flops=15 * 10**9, bytes_accessed=10 * 2**20, transcendentals=2 * 10**6
        ),
    )(
        tokens, cotangent, segments[None], jnp.asarray(frequencies()), gu_in, w_down[0], w_qkv[0], w_out[0], vec,
        jnp.asarray(pad_matrix()),
    )
    rows = lambda array: array.transpose(1, 0, 2)
    return (
        states[None], igrads[None], rows(oqkv), b_grad, rows(oout), ga_grad, gm_grad,
        from_rank(ogu[:, :, :FP]), from_rank(ogu[:, :, FP:]), rows(od),
    )


def solution(mesh):
    return jax.shard_map(
        body,
        mesh=mesh,
        in_specs=(
            P("fsdp", None),
            P("fsdp"),
            P("fsdp", None),
            P("section", "fsdp", None),
            P("section", "fsdp"),
            P("section", "fsdp", None),
            P("section", "fsdp"),
            P("section", "fsdp"),
            P("section", "fsdp", None),
            P("section", "fsdp", None),
            P("section", "fsdp", None),
        ),
        out_specs=(
            P("section", "fsdp", None),
            P("section", "fsdp", None),
            P("section", "fsdp", None),
            P("section", "fsdp"),
            P("section", "fsdp", None),
            P("section", "fsdp"),
            P("section", "fsdp"),
            P("section", "fsdp", None),
            P("section", "fsdp", None),
            P("section", "fsdp", None),
        ),
        check_vma=False,
    )
```

```python
import functools

import jax
import jax.numpy as jnp
import numpy as np
from jax import lax
from jax.experimental import pallas as pl
from jax.experimental.pallas import tpu as pltpu
from jax.sharding import PartitionSpec as P

D = 896
QH = 14
KVH = 2
HD = 64
FF = 4864
QKV = 1152
ROWS = 64
TOK = 128
RING = 4

DP = 1024
FP = 1280
ATT = QKV + DP
N_SEM = 160

eps_norm = 1e-06
theta_base = 1000000.0
MESH = pl.DeviceIdType.MESH
F32 = jnp.float32
BF16 = jnp.bfloat16


def dot(left, right):
    return jnp.dot(left, right, preferred_element_type=F32)


def dot_back(left, right):
    return lax.dot_general(left, right, (((1,), (1,)), ((), ())), preferred_element_type=F32)


def dot_rows(left, right):
    return lax.dot_general(left, right, (((0,), (0,)), ((), ())), preferred_element_type=F32)


def times(n, step):
    def run(i, carry):
        step(i)
        return carry

    lax.fori_loop(0, n, run, 0)


def span(start, size, unit):
    return pl.ds(pl.multiple_of(start, unit), size)


def up1(c):
    return lax.rem(c + 1, RING)


def up2(c):
    return lax.rem(c + 2, RING)


def up3(c):
    return lax.rem(c + 3, RING)


WHOLE = slice(None)
BY_AXES = (("z", "x", "y"), ("y", "z", "x"), ("x", "y", "z"))


def first_whole(index, i):
    k = index.index(WHOLE)
    return index[:k] + (i,) + index[k + 1 :]


def kernel(
    tok, cot, seg, freq, gu_in, d_in, qkv_in, out_in, vec, pad_s,
    states, igrads, ogu, od, oqkv, oout, ob, oga, ogm,
    w_att, w_gu, w_d, g_out, g_qkv,
    xin, dyin, ybuf, dxbuf, h1, obuf, do_buf, datt, dp_buf, h1t, ot,
    h2all, dmall, gact, aact, dgu, h2t, at,
    part_f, part_b, sum_f, sum_b, dh,
    u1, u2, x1, proj, qs, kd, vd, probs, norms,
    gu1, gu2, gu3, gu4, d1, d2, d3, out1, out2, out3, qkv1, qkv2, qkv3,
    cos_t, sin_t, mask, send, recv, turn,
):
    sec = lax.axis_index("section")
    me = lax.axis_index("fsdp")
    at_axis = {"z": me // 16, "x": lax.rem(me // 4, 4), "y": lax.rem(me, 4)}
    z, x, y = at_axis["z"], at_axis["x"], at_axis["y"]

    def device(axis, c):
        place = dict(at_axis)
        place[axis] = c
        return (sec, place["z"] * 16 + place["x"] * 4 + place["y"])

    other = (1 - sec, me)
    barrier = pltpu.get_barrier_semaphore()
    partners = [device(axis, step(at_axis[axis])) for axis in "zxy" for step in (up1, up3, up2)]
    partners.append(other)
    for dev in partners:
        pl.semaphore_signal(barrier, inc=1, device_id=dev, device_id_type=MESH)

    count = [0]
    pending = []

    def remote(src, dst, dev):
        k = count[0]
        count[0] += 1
        return pltpu.make_async_remote_copy(
            src_ref=src, dst_ref=dst, send_sem=send.at[k], recv_sem=recv.at[k],
            device_id=dev, device_id_type=MESH,
        )

    late = []

    def go(cp, pool=pending):
        cp.start()
        if not any(cp is seen for seen in pool):
            pool.append(cp)

    class RingGather:
        def __init__(self, ref, index, cols, cut, axis):
            c = at_axis[axis]
            lo, hi = cols
            whole = lambda k: ref.at[index(k) + (WHOLE, pl.ds(lo, hi - lo))]
            left = lambda k: ref.at[index(k) + (WHOLE, pl.ds(lo, cut - lo))]
            right = lambda k: ref.at[index(k) + (WHOLE, pl.ds(cut, hi - cut))]
            up, down = device(axis, up1(c)), device(axis, up3(c))
            self.a = remote(whole(c), whole(c), up)
            self.b = remote(whole(c), whole(c), down)
            self.e = remote(left(up3(c)), left(up3(c)), up)
            self.f = remote(right(up1(c)), right(up1(c)), down)

        def start(self):
            go(self.a)
            go(self.b)

        def mid(self):
            self.a.wait_recv()
            go(self.e)
            self.b.wait_recv()
            go(self.f)

        def end(self):
            self.e.wait_recv()
            self.f.wait_recv()

    class Gather:
        def __init__(self, ref, index, cols, axis):
            c = at_axis[axis]
            block = ref.at[index(c) + (WHOLE, pl.ds(cols[0], cols[1] - cols[0]))]
            self.copies = [remote(block, block, device(axis, step(c))) for step in (up1, up3, up2)]

        def start(self):
            for cp in self.copies:
                go(cp)

        def end(self):
            for cp in self.copies:
                cp.wait_recv()

    class RingReduce:
        def __init__(self, ref, index, cols, axis, r1, r2):
            c = at_axis[axis]
            lo, hi = cols
            cut = (lo + hi) // 2
            self.ref, self.index, self.c, self.r1, self.r2 = ref, index, c, r1, r2
            self.whole = pl.ds(lo, hi - lo)
            self.left, self.right = pl.ds(lo, cut - lo), pl.ds(cut, hi - cut)
            view = lambda k, part: ref.at[index(k) + (WHOLE, part)]
            up, down = device(axis, up1(c)), device(axis, up3(c))
            self.a = remote(view(up2(c), self.left), r1.at[0], up)
            self.b = remote(view(up2(c), self.right), r1.at[1], down)
            self.e = remote(view(up1(c), self.whole), r2.at[0], up)
            self.f = remote(view(up3(c), self.whole), r2.at[1], down)

        def start(self):
            go(self.a)
            go(self.b)

        def add(self, k, cols, slot):
            def step(i):
                here = first_whole(self.index(k), i) + (WHOLE, cols)
                self.ref[here] = (
                    self.ref[here].astype(F32) + self.r1[slot, i].astype(F32)).astype(BF16)

            times(RING, step)

        def mid(self):
            self.a.wait_recv()
            self.add(up1(self.c), self.left, 0)
            go(self.e)
            self.b.wait_recv()
            self.add(up3(self.c), self.right, 1)
            go(self.f)

        def end(self):
            self.e.wait_recv()
            self.f.wait_recv()

            def step(i):
                here = first_whole(self.index(self.c), i) + (WHOLE, self.whole)
                self.ref[here] = (
                    self.ref[here].astype(F32) + self.r2[0, i].astype(F32) + self.r2[1, i].astype(F32)
                ).astype(BF16)

            times(RING, step)

    class Reduce:
        def __init__(self, ref, index, cols, axis, r):
            c = at_axis[axis]
            part = pl.ds(cols[0], cols[1] - cols[0])
            self.ref, self.r, self.here = ref, r, index(c) + (WHOLE, part)
            self.copies = [
                remote(ref.at[index(step(c)) + (WHOLE, part)], r.at[k], device(axis, step(c)))
                for k, step in enumerate((up1, up3, up2))
            ]

        def start(self):
            for cp in self.copies:
                go(cp)

        def total(self):
            for cp in self.copies:
                cp.wait_recv()
            return self.ref[self.here].astype(F32) + (
                self.r[0].astype(F32) + self.r[1].astype(F32) + self.r[2].astype(F32))

        def end(self):
            self.ref[self.here] = self.total().astype(BF16)

    class TokenGather:
        def __init__(self, ref, pool):
            self.pool = pool
            up, down = device("y", up1(y)), device("y", up3(y))
            self.a = remote(ref.at[0], ref.at[1], up)
            self.b = remote(ref.at[0], ref.at[2], down)
            left, right = pl.ds(0, 512), pl.ds(512, 512)
            self.e = remote(ref.at[1, :, left], ref.at[3, :, left], up)
            self.f = remote(ref.at[2, :, right], ref.at[3, :, right], down)

        def start(self):
            go(self.a, self.pool)
            go(self.b, self.pool)

        def mid(self):
            self.a.wait_recv()
            go(self.e, self.pool)
            self.b.wait_recv()
            go(self.f, self.pool)

        def end(self):
            self.e.wait_recv()
            self.f.wait_recv()

    def gathered(order, phase):
        done = order[:phase]
        return lambda c: tuple(
            WHOLE if a in done else c if a == order[phase] else at_axis[a] for a in ("z", "x", "y"))

    def reduced(order, phase):
        done = order[:phase]
        return lambda c: tuple(
            at_axis[a] if a in done else c if a == order[phase] else WHOLE for a in ("z", "x", "y"))

    mine = pl.ds(pl.multiple_of(16 * y, 16), 16)

    to_rank = [
        remote(gu_in.at[step(y)], w_gu.at[z, x, mine], device("y", step(y))) for step in (up1, up3, up2)]
    gate_x = Gather(w_gu, lambda c: (z, c), (0, FP), "x")
    gate_z = RingGather(w_gu, lambda c: (c, WHOLE), (0, FP), FP // 2, "z")
    up_z = Gather(w_gu, lambda c: (c, x), (FP, 2 * FP), "z")
    up_x = RingGather(w_gu, lambda c: (WHOLE, c), (FP, 2 * FP), FP + FP // 2, "x")
    low_x = Gather(w_d, lambda c: (c, z), (0, 512), "x")
    low_z = RingGather(w_d, lambda c: (WHOLE, c), (0, 512), 256, "z")
    high_z = Gather(w_d, lambda c: (x, c), (512, DP), "z")
    high_x = RingGather(w_d, lambda c: (c, WHOLE), (512, DP), 768, "x")
    att_cols = ((0, QKV), (QKV, QKV + 512), (QKV + 512, ATT))
    att_cut = (640, QKV + 256, QKV + 768)
    att_0 = [Gather(w_att, gathered(o, 0), c, o[0]) for o, c in zip(BY_AXES, att_cols)]
    att_1 = [Gather(w_att, gathered(o, 1), c, o[1]) for o, c in zip(BY_AXES, att_cols)]
    att_2 = [
        RingGather(w_att, gathered(o, 2), c, k, o[2]) for o, c, k in zip(BY_AXES, att_cols, att_cut)]

    pl.semaphore_wait(barrier, len(partners))
    for cp in to_rank:
        go(cp)

    w_gu[z, x, mine, :] = gu_in[y]

    def placed(n, width):
        source = lax.broadcasted_iota(jnp.int32, (128, width), 0)
        target = lax.broadcasted_iota(jnp.int32, (128, width), 1)
        return jnp.where((target == source + n * me) & (source < n), 1.0, 0.0).astype(BF16)

    x1[0:76, pl.ds(0, D)] = d_in[...].astype(F32)
    x1[76:80, pl.ds(0, D)] = jnp.zeros((4, D), F32)
    w_d[x, z] = dot(x1[0:80, pl.ds(0, D)].astype(BF16), pad_s[...]).astype(BF16)
    bias = dot(vec[...], placed(18, QKV))
    gains = dot(vec[...], placed(14, D))
    proj[0:14, :] = qkv_in[...].astype(F32)
    proj[14:15, :] = bias[0:1]
    proj[15:16, pl.ds(0, D)] = gains[1:2]
    proj[15:16, pl.ds(D, QKV - D)] = jnp.zeros((1, QKV - D), F32)
    w_att[z, x, y, :, :QKV] = proj[0:16, :].astype(BF16)
    u1[0:14, pl.ds(0, D)] = out_in[...].astype(F32)
    u1[14:15, pl.ds(0, D)] = gains[2:3]
    u1[15:16, pl.ds(0, D)] = jnp.zeros((1, D), F32)
    w_att[z, x, y, :, QKV:] = dot(u1[0:16, pl.ds(0, D)].astype(BF16), pad_s[...]).astype(BF16)

    for g in att_0:
        g.start()
    low_x.start()
    high_z.start()

    for cp in to_rank:
        cp.wait_recv()

    @pl.when(sec == 1)
    def _():
        pl.semaphore_wait(turn, 1)

    gate_x.start()
    up_z.start()

    row_no = lax.broadcasted_iota(jnp.int32, (TOK, TOK), 0)
    col_no = lax.broadcasted_iota(jnp.int32, (TOK, TOK), 1)
    seg_j = jnp.broadcast_to(seg[...].astype(F32), (TOK, TOK))
    seg_i = seg_j.T
    same_block = jnp.where(row_no < ROWS, 0, 1) == jnp.where(col_no < ROWS, 0, 1)
    earlier = jnp.sum(
        jnp.where(same_block & (seg_j < seg_i), 1.0, 0.0), axis=1, keepdims=True)
    place = jnp.where(row_no < ROWS, row_no, row_no - ROWS).astype(F32) - earlier
    angles = place * freq[0:1]
    cos_t[...] = jnp.cos(angles)
    sin_t[...] = jnp.sin(angles) * freq[1:2]
    mask[...] = jnp.where(same_block & (seg_j == seg_i) & (col_no <= row_no), 1.0, 0.0)
    for g, after in zip(att_0, att_1):
        g.end()
        after.start()
    gate_x.end()
    gate_z.start()
    up_z.end()
    up_x.start()
    for g, after in zip(att_1, att_2):
        g.end()
        after.start()
    low_x.end()
    high_z.end()
    low_z.start()
    high_x.start()
    for g in att_2:
        g.mid()
    gate_z.mid()
    up_x.mid()
    low_z.mid()
    high_x.mid()

    @pl.when(sec == 0)
    def _():
        pl.semaphore_signal(turn, inc=1, device_id=other, device_id_type=MESH)

    att_2[0].end()

    send_y = remote(ybuf, xin, other)
    send_dx = remote(dxbuf, dyin, other)
    dmg = TokenGather(dmall, late)

    @pl.when(sec == 0)
    def _():
        xin[...] = dot(tok[...], pad_s[...]).astype(BF16)

    @pl.when(sec == 1)
    def _():
        dyin[...] = dot(cot[...], pad_s[...]).astype(BF16)
        dmall[0] = dyin[...]
        dmg.start()
        send_y.wait_recv()

    lanes = lax.broadcasted_iota(jnp.int32, (TOK, DP), 1)
    slot = lax.rem(lanes, 16)
    picks = lax.rem(lax.broadcasted_iota(jnp.int32, (8, DP), 1), 16)
    pick15 = jnp.where(picks == 15, 1.0, 0.0).astype(BF16)
    pick14 = jnp.where(picks == 14, 1.0, 0.0).astype(BF16)
    lane = lax.broadcasted_iota(jnp.int32, (TOK, 128), 1)
    low_half = lane < HD
    first = lax.rem(lane, HD) < HD // 2

    def att_weight(start, size):
        return w_att[:, :, :, :, pl.ds(start, size)].reshape(DP, size)

    def swap(tile):
        return jnp.where(first, pltpu.roll(tile, 96, 1), pltpu.roll(tile, 32, 1))

    stream = xin[...].astype(F32)
    inv1 = lax.rsqrt(jnp.sum(stream * stream, axis=1, keepdims=True) * (1.0 / D) + eps_norm)
    norms[0] = inv1
    gains = dot(pick15, att_weight(0, D)).astype(BF16)
    gain_a = dot(gains, pad_s[...])[0:1]
    unit1 = stream * inv1
    u1[...] = unit1
    h1[...] = jnp.where(slot == 14, 1.0, unit1 * gain_a).astype(BF16)
    for i in range(3):
        proj[:, pl.ds(384 * i, 384)] = dot(h1[...], att_weight(384 * i, 384))

    def rotated(j):
        tile = proj[:, pl.ds(128 * j, 128)]
        return tile * cos_t[...] + swap(tile) * sin_t[...]

    def both(tile):
        rolled = pltpu.roll(tile, HD, 1)
        return (
            jnp.where(low_half, tile, rolled).astype(BF16),
            jnp.where(low_half, rolled, tile).astype(BF16),
        )

    def keep(head):
        return low_half if head % 2 == 0 else ~low_half

    kd[0], kd[1] = both(rotated(7))
    vd[0], vd[1] = both(proj[:, pl.ds(1024, 128)])
    allowed = mask[...] > 0.5
    for t in range(7):
        tile = rotated(t)
        outs = []
        for head in (2 * t, 2 * t + 1):
            kv = head // 7
            q = jnp.where(keep(head), tile, 0.0).astype(BF16)
            qs[head] = q
            s = dot_back(q, kd[kv]) * HD ** (-0.5)
            s = jnp.where(allowed, s, -1e30)
            weights = jnp.exp(s - jnp.max(s, axis=1, keepdims=True))
            pr = weights / jnp.sum(weights, axis=1, keepdims=True)
            probs[head] = pr
            outs.append(dot(pr.astype(BF16), vd[kv]))
        dp_buf[:, pl.ds(128 * t, 128)] = jnp.where(low_half, outs[0], outs[1]).astype(BF16)
    obuf[...] = dot(dp_buf[:, pl.ds(0, D)], pad_s[...]).astype(BF16)
    att_2[1].end()
    att_2[2].end()
    gain_m = dot(pick14, att_weight(QKV, DP))[0:1]
    for i in range(4):
        cols = pl.ds(256 * i, 256)
        x1[:, cols] = xin[:, cols].astype(F32) + dot(obuf[...], att_weight(QKV + 256 * i, 256))
    middle = x1[...]
    inv2 = lax.rsqrt(jnp.sum(middle * middle, axis=1, keepdims=True) * (1.0 / D) + eps_norm)
    norms[1] = inv2
    unit2 = middle * inv2
    u2[...] = unit2
    h2all[0] = (unit2 * gain_m).astype(BF16)

    def token_sums(part, sums):
        return [
            remote(part.at[1], sums.at[0], device("y", up3(y))),
            remote(part.at[2], sums.at[1], device("y", up1(y))),
            remote(part.at[3], sums.at[2], device("y", up2(y))),
        ]

    def token_total(part, sums, copies):
        for cp in copies:
            cp.wait_recv()
        return part[0].astype(F32) + (
            sums[0].astype(F32) + sums[1].astype(F32) + sums[2].astype(F32))

    def mlp(k, n):
        rows = n * TOK
        for i in range(5):
            cols, cols_up = pl.ds(256 * i, 256), pl.ds(FP + 256 * i, 256)
            h = h2all[k : k + n].reshape(rows, DP)
            gate = dot(h, w_gu[:, :, :, cols].reshape(DP, 256))
            upward = dot(h, w_gu[:, :, :, cols_up].reshape(DP, 256))
            gact[k : k + n, :, cols] = gate.reshape(n, TOK, 256)
            gact[k : k + n, :, cols_up] = upward.reshape(n, TOK, 256)
            aact[k : k + n, :, cols] = (
                gate * jax.nn.sigmoid(gate) * upward).astype(BF16).reshape(n, TOK, 256)
        for i in range(4):
            cols = pl.ds(256 * i, 256)
            a = aact[k : k + n].reshape(rows, FP)
            part_f[k : k + n, :, cols] = dot(
                a, w_d[:, :, :, cols].reshape(FP, 256)).astype(BF16).reshape(n, TOK, 256)

    ag = TokenGather(h2all, pending)
    sums = token_sums(part_f, sum_f)
    ag.start()

    @pl.when(sec == 1)
    def _():
        dmg.mid()

    gate_z.end()
    up_x.end()
    low_z.end()
    high_x.end()

    mlp(0, 1)
    ag.mid()
    mlp(1, 2)
    go(sums[0])
    go(sums[1])
    ag.end()
    mlp(3, 1)
    go(sums[2])
    for c in range(RING):
        cols = pl.ds(128 * c, 128)
        h2t[:, cols] = h2all[c].T
        at[:, cols] = aact[c].T
    h1t[...] = h1[...].T
    ot[...] = obuf[...].T
    out = x1[...] + token_total(part_f, sum_f, sums)
    for cp in pending:
        cp.wait_send()
    pending.clear()
    ybuf[...] = out.astype(BF16)

    @pl.when(sec == 0)
    def _():
        send_y.start()


    def store_states():
        states[...] = dot_back(ybuf[...], pad_s[...]).astype(BF16)

    @pl.when(sec == 0)
    def _():
        store_states()
        send_dx.wait_recv()
        dmall[0] = dyin[...]
        dmg.start()

    def mlp_back(k, n):
        rows = n * TOK
        for i in range(2):
            cols, cols_up = pl.ds(640 * i, 640), pl.ds(FP + 640 * i, 640)
            da = dot_back(dmall[k : k + n].reshape(rows, DP), w_d[2 * i : 2 * i + 2].reshape(640, DP))
            gate = gact[k : k + n, :, cols].reshape(rows, 640)
            upward = gact[k : k + n, :, cols_up].reshape(rows, 640)
            sig = jax.nn.sigmoid(gate)
            dgate = da * upward * (sig * (1.0 + gate * (1.0 - sig)))
            dgu[k : k + n, :, cols] = dgate.astype(BF16).reshape(n, TOK, 640)
            dgu[k : k + n, :, cols_up] = (da * gate * sig).astype(BF16).reshape(n, TOK, 640)
        for i in range(4):
            cols = pl.ds(256 * i, 256)
            part_b[k : k + n, :, cols] = dot_back(
                dgu[k : k + n].reshape(rows, 2 * FP), w_gu[i].reshape(256, 2 * FP)
            ).astype(BF16).reshape(n, TOK, 256)

    sums = token_sums(part_b, sum_b)
    mlp_back(0, 1)

    @pl.when(sec == 0)
    def _():
        dmg.mid()

    mlp_back(1, 2)
    go(sums[0])
    go(sums[1])
    dmg.end()
    mlp_back(3, 1)
    go(sums[2])

    rgate_z = RingReduce(w_gu, lambda c: (c, WHOLE), (0, FP), "z", gu1.at[0], gu2.at[0])
    rup_x = RingReduce(w_gu, lambda c: (WHOLE, c), (FP, 2 * FP), "x", gu1.at[1], gu2.at[1])
    rgate_x = Reduce(w_gu, lambda c: (z, c), (0, FP), "x", gu3.at[0])
    rup_z = Reduce(w_gu, lambda c: (c, x), (FP, 2 * FP), "z", gu3.at[1])
    rlow_z = RingReduce(w_d, lambda c: (WHOLE, c), (0, 512), "z", d1.at[0], d2.at[0])
    rhigh_x = RingReduce(w_d, lambda c: (c, WHOLE), (512, DP), "x", d1.at[1], d2.at[1])
    rlow_x = Reduce(w_d, lambda c: (c, z), (0, 512), "x", d3.at[0])
    rhigh_z = Reduce(w_d, lambda c: (x, c), (512, DP), "z", d3.at[1])
    from_rank = [
        remote(
            w_gu.at[z, x, pl.ds(pl.multiple_of(16 * step(y), 16), 16)],
            gu4.at[y], device("y", step(y)))
        for step in (up1, up3, up2)
    ]
    out_red = [
        Reduce(g_out, reduced("yxz", k), (0, DP), "yxz"[k], r) for k, r in enumerate((out1, out2, out3))]
    qkv_order = ("yxz", "xzy", "zyx")
    qkv_red = [
        [
            Reduce(g_qkv, reduced(order, k), (384 * n, 384 * n + 384), order[k], r.at[n])
            for n, order in enumerate(qkv_order)
        ]
        for k, r in enumerate((qkv1, qkv2, qkv3))
    ]

    def gu_terms():
        def grad_gate(i):
            rows = span(256 * i, 256, 256)
            g = dot(h2t[rows, :], dgu[:, :, pl.ds(0, FP)].reshape(512, FP))
            w_gu[i, :, :, pl.ds(0, FP)] = g.astype(BF16).reshape(4, 64, FP)

        def grad_up(i):
            rows = span(256 * i, 256, 256)
            g = dot(h2t[rows, :], dgu[:, :, pl.ds(FP, FP)].reshape(512, FP))
            w_gu[i, :, :, pl.ds(FP, FP)] = g.astype(BF16).reshape(4, 64, FP)

        times(4, grad_gate)
        rgate_z.start()
        times(4, grad_up)
        rup_x.start()

    def d_terms():
        def grad_d(i):
            rows = span(320 * i, 320, 64)
            g = dot(at[rows, :], dmall[...].reshape(512, DP))
            w_d[i] = g.astype(BF16).reshape(4, 80, DP)

        times(4, grad_d)
        rlow_z.start()
        rhigh_x.start()

    row = lax.rem(lax.broadcasted_iota(jnp.int32, (256, 384), 0), 16)

    def out_terms():
        def grad(i):
            g = dot(ot[span(256 * i, 256, 256), :], datt[...])
            g = jnp.where(row14, dh[0:1, :], g)
            g_out[i] = g.astype(BF16).reshape(4, 4, 16, DP)

        row14 = lax.rem(lax.broadcasted_iota(jnp.int32, (256, DP), 0), 16) == 14
        times(4, grad)
        out_red[0].start()

    gu_terms()

    @pl.when(sec == 0)
    def _():
        d_terms()

    dh2 = token_total(part_b, sum_b, sums)
    unit2 = u2[...]
    dh[0:1, :] = jnp.sum(dh2 * unit2, axis=0, keepdims=True)
    gained = dh2 * gain_m
    dx1 = dyin[...].astype(F32) + norms[1] * (
        gained - unit2 * (jnp.sum(gained * unit2, axis=1, keepdims=True) * (1.0 / D)))
    x1[...] = dx1
    datt[...] = dx1.astype(BF16)

    @pl.when(sec == 0)
    def _():
        out_terms()

    for i in range(4):
        w = w_att[i, :, :, :, pl.ds(QKV, DP)].reshape(256, DP)
        do_buf[:, pl.ds(256 * i, 256)] = dot_back(datt[...], w).astype(BF16)
    proj[:, pl.ds(0, D)] = dot_back(do_buf[...], pad_s[...])

    def unrotated(tile):
        return (tile * cos_t[...] - swap(tile) * sin_t[...]).astype(BF16)

    dk_sum = [jnp.zeros((TOK, 128), F32)] * 2
    dv_sum = [jnp.zeros((TOK, 128), F32)] * 2
    for t in range(7):
        tile = proj[:, pl.ds(128 * t, 128)]
        dqs = []
        for head in (2 * t, 2 * t + 1):
            kv = head // 7
            do_h = jnp.where(keep(head), tile, 0.0).astype(BF16)
            pr = probs[head]
            dpr = dot_back(do_h, vd[kv])
            ds = (pr * (dpr - jnp.sum(dpr * pr, axis=1, keepdims=True))).astype(BF16)
            dv_sum[kv] = dv_sum[kv] + dot_rows(pr.astype(BF16), do_h)
            dk_sum[kv] = dk_sum[kv] + dot_rows(ds, qs[head])
            dqs.append(dot(ds, kd[kv]) * HD ** (-0.5))
        dp_buf[:, pl.ds(128 * t, 128)] = unrotated(jnp.where(low_half, dqs[0], dqs[1]))
    dk_sum = [(dk + pltpu.roll(dk, HD, 1)) * HD ** (-0.5) for dk in dk_sum]
    dv_sum = [dv + pltpu.roll(dv, HD, 1) for dv in dv_sum]
    dp_buf[:, pl.ds(896, 128)] = unrotated(jnp.where(low_half, dk_sum[0], dk_sum[1]))
    dp_buf[:, pl.ds(1024, 128)] = jnp.where(low_half, dv_sum[0], dv_sum[1]).astype(BF16)
    rgate_z.mid()
    rup_x.mid()
    for i in range(4):
        w = w_att[i, :, :, :, pl.ds(0, QKV)].reshape(256, QKV)
        proj[:, pl.ds(256 * i, 256)] = dot_back(dp_buf[...], w)
    dh1 = jnp.where(slot < 14, proj[:, pl.ds(0, DP)], 0.0)
    unit1 = u1[...]
    dgain_a = jnp.sum(dh1 * unit1, axis=0, keepdims=True)

    def qkv_terms():
        proj[0:1, pl.ds(0, DP)] = dgain_a
        for n in range(3):
            cols = pl.ds(384 * n, 384)

            def grad(i, cols=cols):
                g = dot(h1t[span(256 * i, 256, 256), :], dp_buf[:, cols])
                g = jnp.where(row == 15, proj[0:1, cols], g)
                g_qkv[i, :, :, :, cols] = g.astype(BF16).reshape(4, 4, 16, 384)

            times(4, grad)
            qkv_red[0][n].start()

    @pl.when(sec == 0)
    def _():
        qkv_terms()

    gained = dh1 * gain_a
    dx = x1[...] + norms[0] * (
        gained - unit1 * (jnp.sum(gained * unit1, axis=1, keepdims=True) * (1.0 / D)))
    dx_hi = dx.astype(BF16)
    dxbuf[...] = dx_hi

    @pl.when(sec == 1)
    def _():
        send_dx.start()
        igrads[...] = dot_back(dx_hi, pad_s[...])
        d_terms()
        out_terms()
        qkv_terms()
        store_states()

    @pl.when(sec == 0)
    def _():
        dx_lo = (dx - dx_hi.astype(F32)).astype(BF16)
        igrads[...] = dot_back(dx_hi, pad_s[...]) + dot_back(dx_lo, pad_s[...])

    rlow_z.mid()
    rhigh_x.mid()
    rgate_z.end()
    rgate_x.start()
    rup_x.end()
    rup_z.start()
    out_red[0].end()
    out_red[1].start()
    for red, after in zip(qkv_red[0], qkv_red[1]):
        red.end()
        after.start()
    rlow_z.end()
    rlow_x.start()
    rhigh_x.end()
    rhigh_z.start()
    out_red[1].end()
    out_red[2].start()
    rgate_x.end()
    rup_z.end()
    for cp in from_rank:
        go(cp)
    for red, after in zip(qkv_red[1], qkv_red[2]):
        red.end()
        after.start()

    def unpadded(total):
        hi = total.astype(BF16)
        lo = (total - hi.astype(F32)).astype(BF16)
        return dot_back(hi, pad_s[...]) + dot_back(lo, pad_s[...])

    def own_lanes(rows, n):
        width = rows.shape[1]
        target = lax.broadcasted_iota(jnp.int32, (width, 128), 1)
        source = lax.broadcasted_iota(jnp.int32, (width, 128), 0)
        move = jnp.where(source == target + n * me, 1.0, 0.0).astype(BF16)
        hi = rows.astype(BF16)
        lo = (rows - hi.astype(F32)).astype(BF16)
        return dot(hi, move) + dot(lo, move)

    def by_row(ref, rows):
        for r in range(ref.shape[0]):
            ref[r] = rows[r : r + 1]

    by_row(od, unpadded(jnp.concatenate([rlow_x.total(), rhigh_z.total()], axis=1)))
    total = unpadded(out_red[2].total())
    by_row(oout, total)
    ogm[...] = own_lanes(total, 14)[14:15, 0:14]
    for n in range(3):
        proj[0:16, pl.ds(384 * n, 384)] = qkv_red[2][n].total()
    by_row(oqkv, proj[0:16, :])
    ob[...] = own_lanes(proj[0:16, :], 18)[14:15, 0:18]
    oga[...] = own_lanes(proj[0:16, pl.ds(0, DP)], 16)[15:16, 0:14]
    ogu[y] = w_gu[z, x, mine, :]
    for cp in from_rank:
        cp.wait_recv()
    for step in (up1, up3, up2):
        ogu[step(y)] = gu4[step(y)]

    for cp in pending + late:
        cp.wait_send()

    @pl.when(sec == 0)
    def _():
        send_y.wait_send()

    @pl.when(sec == 1)
    def _():
        send_dx.wait_send()


def pad_matrix():
    column = np.arange(DP)
    row = np.where(column % 16 < 14, 14 * (column // 16) + column % 16, -1)
    return (np.arange(D)[:, None] == row[None, :]).astype(jnp.bfloat16)


def frequencies():
    half = HD // 2
    inverse = theta_base ** (-(np.arange(half, dtype=np.float64) * 2.0 / HD))
    sign = np.where(np.arange(128) % HD < half, -1.0, 1.0)
    return np.concatenate([np.tile(inverse, 4)[None], sign[None], np.zeros((6, 128))]).astype(np.float32)


def by_rank(weight):
    pieces = weight.reshape(14, 4, 4, 4, 76).transpose(3, 0, 2, 1, 4)
    return jnp.pad(pieces, ((0, 0), (0, 2), (0, 0), (0, 0), (0, 4))).reshape(4, 16, FP)


def from_rank(grad):
    pieces = grad.reshape(4, 16, 4, 4, 80)[:, :14, :, :, :76]
    return pieces.transpose(1, 3, 2, 0, 4).reshape(1, 14, FF).astype(F32)


def body(
    tokens, segments, cotangent, w_qkv, b_qkv, w_out, gain_attn, gain_mlp, w_gate, w_up, w_down
):
    gu_in = jnp.concatenate([by_rank(w_gate[0]), by_rank(w_up[0])], axis=2)
    vec = jnp.concatenate(
        [jnp.pad(v, ((0, 0), (0, 128 - v.shape[1]))) for v in (b_qkv, gain_attn, gain_mlp)]
        + [jnp.zeros((13, 128), BF16)])
    sds = jax.ShapeDtypeStruct
    vm = pltpu.VMEM
    states, igrads, ogu, od, oqkv, oout, b_grad, ga_grad, gm_grad = pl.pallas_call(
        kernel,
        out_shape=(
            sds((TOK, D), BF16), sds((TOK, D), F32), sds((4, 16, 2 * FP), BF16),
            sds((76, 1, D), F32), sds((14, 1, QKV), F32), sds((14, 1, D), F32),
            sds((1, 18), F32), sds((1, 14), F32), sds((1, 14), F32),
        ),
        in_specs=[pl.BlockSpec(memory_space=pltpu.VMEM)] * 10,
        out_specs=tuple([pl.BlockSpec(memory_space=pltpu.VMEM)] * 9),
        scratch_shapes=[
            vm((4, 4, 4, 16, ATT), BF16), vm((4, 4, 64, 2 * FP), BF16), vm((4, 4, 80, DP), BF16),
            vm((4, 4, 4, 16, DP), BF16), vm((4, 4, 4, 16, QKV), BF16),
            *[vm((TOK, DP), BF16)] * 8, vm((TOK, QKV), BF16), vm((DP, TOK), BF16), vm((DP, TOK), BF16),
            vm((4, TOK, DP), BF16), vm((4, TOK, DP), BF16), vm((4, TOK, 2 * FP), F32),
            vm((4, TOK, FP), BF16), vm((4, TOK, 2 * FP), BF16), vm((DP, 512), BF16), vm((FP, 512), BF16),
            vm((4, TOK, DP), BF16), vm((4, TOK, DP), BF16),
            vm((3, TOK, DP), BF16), vm((3, TOK, DP), BF16), vm((8, DP), F32),
            vm((TOK, DP), F32), vm((TOK, DP), F32), vm((TOK, DP), F32), vm((TOK, QKV), F32),
            vm((QH, TOK, 128), BF16), vm((2, TOK, 128), BF16), vm((2, TOK, 128), BF16),
            vm((QH, TOK, 128), F32), vm((2, TOK, 1), F32),
            vm((2, 2, 4, 64, FP // 2), BF16), vm((2, 2, 4, 64, FP), BF16),
            vm((2, 3, 64, FP), BF16), vm((4, 16, 2 * FP), BF16),
            vm((2, 2, 4, 80, 256), BF16), vm((2, 2, 4, 80, 512), BF16), vm((2, 3, 80, 512), BF16),
            vm((3, 4, 4, 16, DP), BF16), vm((3, 4, 16, DP), BF16), vm((3, 16, DP), BF16),
            vm((3, 3, 4, 4, 16, 384), BF16), vm((3, 3, 4, 16, 384), BF16), vm((3, 3, 16, 384), BF16),
            *[vm((TOK, TOK), F32)] * 3,
            pltpu.SemaphoreType.DMA((N_SEM,)), pltpu.SemaphoreType.DMA((N_SEM,)),
            pltpu.SemaphoreType.REGULAR,
        ],
        compiler_params=pltpu.CompilerParams(
            collective_id=0, has_side_effects=True, vmem_limit_bytes=60 * 2**20
        ),
        cost_estimate=pl.CostEstimate(
            flops=15 * 10**9, bytes_accessed=10 * 2**20, transcendentals=2 * 10**6
        ),
    )(
        tokens, cotangent, segments[None], jnp.asarray(frequencies()), gu_in, w_down[0], w_qkv[0], w_out[0], vec,
        jnp.asarray(pad_matrix()),
    )
    rows = lambda array: array.transpose(1, 0, 2)
    return (
        states[None], igrads[None], rows(oqkv), b_grad, rows(oout), ga_grad, gm_grad,
        from_rank(ogu[:, :, :FP]), from_rank(ogu[:, :, FP:]), rows(od),
    )


def solution(mesh):
    return jax.shard_map(
        body,
        mesh=mesh,
        in_specs=(
            P("fsdp", None),
            P("fsdp"),
            P("fsdp", None),
            P("section", "fsdp", None),
            P("section", "fsdp"),
            P("section", "fsdp", None),
            P("section", "fsdp"),
            P("section", "fsdp"),
            P("section", "fsdp", None),
            P("section", "fsdp", None),
            P("section", "fsdp", None),
        ),
        out_specs=(
            P("section", "fsdp", None),
            P("section", "fsdp", None),
            P("section", "fsdp", None),
            P("section", "fsdp"),
            P("section", "fsdp", None),
            P("section", "fsdp"),
            P("section", "fsdp"),
            P("section", "fsdp", None),
            P("section", "fsdp", None),
            P("section", "fsdp", None),
        ),
        check_vma=False,
    )
```

```python
import functools

import jax
import jax.numpy as jnp
import numpy as np
from jax import lax
from jax.experimental import pallas as pl
from jax.experimental.pallas import tpu as pltpu
from jax.sharding import PartitionSpec as P

D = 896
QH = 14
KVH = 2
HD = 64
FF = 4864
QKV = 1152
ROWS = 64
TOK = 128
RING = 4

DP = 1024
FP = 1280
ATT = QKV + DP
N_SEM = 160

eps_norm = 1e-06
theta_base = 1000000.0
MESH = pl.DeviceIdType.MESH
F32 = jnp.float32
BF16 = jnp.bfloat16


def dot(left, right):
    return jnp.dot(left, right, preferred_element_type=F32)


def dot_back(left, right):
    return lax.dot_general(left, right, (((1,), (1,)), ((), ())), preferred_element_type=F32)


def dot_rows(left, right):
    return lax.dot_general(left, right, (((0,), (0,)), ((), ())), preferred_element_type=F32)


def times(n, step):
    def run(i, carry):
        step(i)
        return carry

    lax.fori_loop(0, n, run, 0)


def span(start, size, unit):
    return pl.ds(pl.multiple_of(start, unit), size)


def up1(c):
    return lax.rem(c + 1, RING)


def up2(c):
    return lax.rem(c + 2, RING)


def up3(c):
    return lax.rem(c + 3, RING)


WHOLE = slice(None)
BY_AXES = (("z", "x", "y"), ("y", "z", "x"), ("x", "y", "z"))


def first_whole(index, i):
    k = index.index(WHOLE)
    return index[:k] + (i,) + index[k + 1 :]


def kernel(
    tok, cot, seg, freq, gu_in, d_in, qkv_in, out_in, vec, pad_s,
    states, igrads, ogate, oup, od, oqkv, oout, ob, oga, ogm,
    w_att, w_gu, w_d, g_out, g_qkv,
    xin, dyin, ybuf, dxbuf, h1, obuf, do_buf, datt, dp_buf, h1t, ot,
    h2all, dmall, gact, aact, dgu, h2t, at,
    part_f, part_b, sum_f, sum_b, dh,
    u1, u2, x1, proj, qs, kd, vd, probs, norms,
    gu1, gu2, gu3, gu4, d1, d2, d3, out1, out2, out3, qkv1, qkv2, qkv3,
    cos_t, sin_t, mask, send, recv, turn,
):
    sec = lax.axis_index("section")
    me = lax.axis_index("fsdp")
    at_axis = {"z": me // 16, "x": lax.rem(me // 4, 4), "y": lax.rem(me, 4)}
    z, x, y = at_axis["z"], at_axis["x"], at_axis["y"]

    def device(axis, c):
        place = dict(at_axis)
        place[axis] = c
        return (sec, place["z"] * 16 + place["x"] * 4 + place["y"])

    other = (1 - sec, me)
    barrier = pltpu.get_barrier_semaphore()
    partners = [device(axis, step(at_axis[axis])) for axis in "zxy" for step in (up1, up3, up2)]
    partners.append(other)
    for dev in partners:
        pl.semaphore_signal(barrier, inc=1, device_id=dev, device_id_type=MESH)

    count = [0]
    pending = []

    def remote(src, dst, dev):
        k = count[0]
        count[0] += 1
        return pltpu.make_async_remote_copy(
            src_ref=src, dst_ref=dst, send_sem=send.at[k], recv_sem=recv.at[k],
            device_id=dev, device_id_type=MESH,
        )

    late = []

    def go(cp, pool=pending):
        cp.start()
        if not any(cp is seen for seen in pool):
            pool.append(cp)

    class RingGather:
        def __init__(self, ref, index, cols, cut, axis):
            c = at_axis[axis]
            lo, hi = cols
            whole = lambda k: ref.at[index(k) + (WHOLE, pl.ds(lo, hi - lo))]
            left = lambda k: ref.at[index(k) + (WHOLE, pl.ds(lo, cut - lo))]
            right = lambda k: ref.at[index(k) + (WHOLE, pl.ds(cut, hi - cut))]
            up, down = device(axis, up1(c)), device(axis, up3(c))
            self.a = remote(whole(c), whole(c), up)
            self.b = remote(whole(c), whole(c), down)
            self.e = remote(left(up3(c)), left(up3(c)), up)
            self.f = remote(right(up1(c)), right(up1(c)), down)

        def start(self):
            go(self.a)
            go(self.b)

        def mid(self):
            self.a.wait_recv()
            go(self.e)
            self.b.wait_recv()
            go(self.f)

        def end(self):
            self.e.wait_recv()
            self.f.wait_recv()

    class Gather:
        def __init__(self, ref, index, cols, axis):
            c = at_axis[axis]
            block = ref.at[index(c) + (WHOLE, pl.ds(cols[0], cols[1] - cols[0]))]
            self.copies = [remote(block, block, device(axis, step(c))) for step in (up1, up3, up2)]

        def start(self):
            for cp in self.copies:
                go(cp)

        def end(self):
            for cp in self.copies:
                cp.wait_recv()

    class RingReduce:
        def __init__(self, ref, index, cols, axis, r1, r2):
            c = at_axis[axis]
            lo, hi = cols
            cut = (lo + hi) // 2
            self.ref, self.index, self.c, self.r1, self.r2 = ref, index, c, r1, r2
            self.whole = pl.ds(lo, hi - lo)
            self.left, self.right = pl.ds(lo, cut - lo), pl.ds(cut, hi - cut)
            view = lambda k, part: ref.at[index(k) + (WHOLE, part)]
            up, down = device(axis, up1(c)), device(axis, up3(c))
            self.a = remote(view(up2(c), self.left), r1.at[0], up)
            self.b = remote(view(up2(c), self.right), r1.at[1], down)
            self.e = remote(view(up1(c), self.whole), r2.at[0], up)
            self.f = remote(view(up3(c), self.whole), r2.at[1], down)

        def start(self):
            go(self.a)
            go(self.b)

        def add(self, k, cols, slot):
            def step(i):
                here = first_whole(self.index(k), i) + (WHOLE, cols)
                self.ref[here] = (
                    self.ref[here].astype(F32) + self.r1[slot, i].astype(F32)).astype(BF16)

            times(RING, step)

        def mid(self):
            self.a.wait_recv()
            self.add(up1(self.c), self.left, 0)
            go(self.e)
            self.b.wait_recv()
            self.add(up3(self.c), self.right, 1)
            go(self.f)

        def end(self):
            self.e.wait_recv()
            self.f.wait_recv()

            def step(i):
                here = first_whole(self.index(self.c), i) + (WHOLE, self.whole)
                self.ref[here] = (
                    self.ref[here].astype(F32) + self.r2[0, i].astype(F32) + self.r2[1, i].astype(F32)
                ).astype(BF16)

            times(RING, step)

    class Reduce:
        def __init__(self, ref, index, cols, axis, r):
            c = at_axis[axis]
            part = pl.ds(cols[0], cols[1] - cols[0])
            self.ref, self.r, self.here = ref, r, index(c) + (WHOLE, part)
            self.copies = [
                remote(ref.at[index(step(c)) + (WHOLE, part)], r.at[k], device(axis, step(c)))
                for k, step in enumerate((up1, up3, up2))
            ]

        def start(self):
            for cp in self.copies:
                go(cp)

        def total(self):
            for cp in self.copies:
                cp.wait_recv()
            return self.ref[self.here].astype(F32) + (
                self.r[0].astype(F32) + self.r[1].astype(F32) + self.r[2].astype(F32))

        def end(self):
            self.ref[self.here] = self.total().astype(BF16)

    class TokenGather:
        def __init__(self, ref, pool):
            self.pool = pool
            up, down = device("y", up1(y)), device("y", up3(y))
            self.a = remote(ref.at[0], ref.at[1], up)
            self.b = remote(ref.at[0], ref.at[2], down)
            left, right = pl.ds(0, 512), pl.ds(512, 512)
            self.e = remote(ref.at[1, :, left], ref.at[3, :, left], up)
            self.f = remote(ref.at[2, :, right], ref.at[3, :, right], down)

        def start(self):
            go(self.a, self.pool)
            go(self.b, self.pool)

        def mid(self):
            self.a.wait_recv()
            go(self.e, self.pool)
            self.b.wait_recv()
            go(self.f, self.pool)

        def end(self):
            self.e.wait_recv()
            self.f.wait_recv()

    def gathered(order, phase):
        done = order[:phase]
        return lambda c: tuple(
            WHOLE if a in done else c if a == order[phase] else at_axis[a] for a in ("z", "x", "y"))

    def reduced(order, phase):
        done = order[:phase]
        return lambda c: tuple(
            at_axis[a] if a in done else c if a == order[phase] else WHOLE for a in ("z", "x", "y"))

    mine = pl.ds(pl.multiple_of(16 * y, 16), 16)

    to_rank = [
        remote(gu_in.at[step(y)], w_gu.at[z, x, mine], device("y", step(y))) for step in (up1, up3, up2)]
    gate_x = Gather(w_gu, lambda c: (z, c), (0, FP), "x")
    gate_z = RingGather(w_gu, lambda c: (c, WHOLE), (0, FP), FP // 2, "z")
    up_z = Gather(w_gu, lambda c: (c, x), (FP, 2 * FP), "z")
    up_x = RingGather(w_gu, lambda c: (WHOLE, c), (FP, 2 * FP), FP + FP // 2, "x")
    low_x = Gather(w_d, lambda c: (c, z), (0, 512), "x")
    low_z = RingGather(w_d, lambda c: (WHOLE, c), (0, 512), 256, "z")
    high_z = Gather(w_d, lambda c: (x, c), (512, DP), "z")
    high_x = RingGather(w_d, lambda c: (c, WHOLE), (512, DP), 768, "x")
    att_cols = ((0, QKV), (QKV, QKV + 512), (QKV + 512, ATT))
    att_cut = (640, QKV + 256, QKV + 768)
    att_0 = [Gather(w_att, gathered(o, 0), c, o[0]) for o, c in zip(BY_AXES, att_cols)]
    att_1 = [Gather(w_att, gathered(o, 1), c, o[1]) for o, c in zip(BY_AXES, att_cols)]
    att_2 = [
        RingGather(w_att, gathered(o, 2), c, k, o[2]) for o, c, k in zip(BY_AXES, att_cols, att_cut)]

    pl.semaphore_wait(barrier, len(partners))
    for cp in to_rank:
        go(cp)

    w_gu[z, x, mine, :] = gu_in[y]

    def placed(n, width):
        source = lax.broadcasted_iota(jnp.int32, (128, width), 0)
        target = lax.broadcasted_iota(jnp.int32, (128, width), 1)
        return jnp.where((target == source + n * me) & (source < n), 1.0, 0.0).astype(BF16)

    x1[0:76, pl.ds(0, D)] = d_in[...].astype(F32)
    x1[76:80, pl.ds(0, D)] = jnp.zeros((4, D), F32)
    w_d[x, z] = dot(x1[0:80, pl.ds(0, D)].astype(BF16), pad_s[...]).astype(BF16)
    bias = dot(vec[...], placed(18, QKV))
    gains = dot(vec[...], placed(14, D))
    proj[0:14, :] = qkv_in[...].astype(F32)
    proj[14:15, :] = bias[0:1]
    proj[15:16, pl.ds(0, D)] = gains[1:2]
    proj[15:16, pl.ds(D, QKV - D)] = jnp.zeros((1, QKV - D), F32)
    w_att[z, x, y, :, :QKV] = proj[0:16, :].astype(BF16)
    u1[0:14, pl.ds(0, D)] = out_in[...].astype(F32)
    u1[14:15, pl.ds(0, D)] = gains[2:3]
    u1[15:16, pl.ds(0, D)] = jnp.zeros((1, D), F32)
    w_att[z, x, y, :, QKV:] = dot(u1[0:16, pl.ds(0, D)].astype(BF16), pad_s[...]).astype(BF16)

    for g in att_0:
        g.start()
    low_x.start()
    high_z.start()

    for cp in to_rank:
        cp.wait_recv()

    @pl.when(sec == 1)
    def _():
        pl.semaphore_wait(turn, 1)

    gate_x.start()
    up_z.start()

    row_no = lax.broadcasted_iota(jnp.int32, (TOK, TOK), 0)
    col_no = lax.broadcasted_iota(jnp.int32, (TOK, TOK), 1)
    seg_j = jnp.broadcast_to(seg[...].astype(F32), (TOK, TOK))
    seg_i = seg_j.T
    same_block = jnp.where(row_no < ROWS, 0, 1) == jnp.where(col_no < ROWS, 0, 1)
    earlier = jnp.sum(
        jnp.where(same_block & (seg_j < seg_i), 1.0, 0.0), axis=1, keepdims=True)
    place = jnp.where(row_no < ROWS, row_no, row_no - ROWS).astype(F32) - earlier
    angles = place * freq[0:1]
    cos_t[...] = jnp.cos(angles)
    sin_t[...] = jnp.sin(angles) * freq[1:2]
    mask[...] = jnp.where(same_block & (seg_j == seg_i) & (col_no <= row_no), 1.0, 0.0)
    for g, after in zip(att_0, att_1):
        g.end()
        after.start()
    gate_x.end()
    gate_z.start()
    up_z.end()
    up_x.start()
    for g, after in zip(att_1, att_2):
        g.end()
        after.start()
    low_x.end()
    high_z.end()
    low_z.start()
    high_x.start()
    for g in att_2:
        g.mid()
    gate_z.mid()
    up_x.mid()
    low_z.mid()
    high_x.mid()

    @pl.when(sec == 0)
    def _():
        pl.semaphore_signal(turn, inc=1, device_id=other, device_id_type=MESH)

    att_2[0].end()

    send_y = remote(ybuf, xin, other)
    send_dx = remote(dxbuf, dyin, other)
    dmg = TokenGather(dmall, late)

    @pl.when(sec == 0)
    def _():
        xin[...] = dot(tok[...], pad_s[...]).astype(BF16)

    @pl.when(sec == 1)
    def _():
        dyin[...] = dot(cot[...], pad_s[...]).astype(BF16)
        dmall[0] = dyin[...]
        dmg.start()
        send_y.wait_recv()

    lanes = lax.broadcasted_iota(jnp.int32, (TOK, DP), 1)
    slot = lax.rem(lanes, 16)
    picks = lax.rem(lax.broadcasted_iota(jnp.int32, (8, DP), 1), 16)
    pick15 = jnp.where(picks == 15, 1.0, 0.0).astype(BF16)
    pick14 = jnp.where(picks == 14, 1.0, 0.0).astype(BF16)
    lane = lax.broadcasted_iota(jnp.int32, (TOK, 128), 1)
    low_half = lane < HD
    first = lax.rem(lane, HD) < HD // 2

    def att_weight(start, size):
        return w_att[:, :, :, :, pl.ds(start, size)].reshape(DP, size)

    def swap(tile):
        return jnp.where(first, pltpu.roll(tile, 96, 1), pltpu.roll(tile, 32, 1))

    stream = xin[...].astype(F32)
    inv1 = lax.rsqrt(jnp.sum(stream * stream, axis=1, keepdims=True) * (1.0 / D) + eps_norm)
    norms[0] = inv1
    gains = dot(pick15, att_weight(0, D)).astype(BF16)
    gain_a = dot(gains, pad_s[...])[0:1]
    unit1 = stream * inv1
    u1[...] = unit1
    h1[...] = jnp.where(slot == 14, 1.0, unit1 * gain_a).astype(BF16)
    for i in range(3):
        proj[:, pl.ds(384 * i, 384)] = dot(h1[...], att_weight(384 * i, 384))

    def rotated(j):
        tile = proj[:, pl.ds(128 * j, 128)]
        return tile * cos_t[...] + swap(tile) * sin_t[...]

    def both(tile):
        rolled = pltpu.roll(tile, HD, 1)
        return (
            jnp.where(low_half, tile, rolled).astype(BF16),
            jnp.where(low_half, rolled, tile).astype(BF16),
        )

    def keep(head):
        return low_half if head % 2 == 0 else ~low_half

    kd[0], kd[1] = both(rotated(7))
    vd[0], vd[1] = both(proj[:, pl.ds(1024, 128)])
    allowed = mask[...] > 0.5
    for t in range(7):
        tile = rotated(t)
        outs = []
        for head in (2 * t, 2 * t + 1):
            kv = head // 7
            q = jnp.where(keep(head), tile, 0.0).astype(BF16)
            qs[head] = q
            s = dot_back(q, kd[kv]) * HD ** (-0.5)
            s = jnp.where(allowed, s, -1e30)
            weights = jnp.exp(s - jnp.max(s, axis=1, keepdims=True))
            pr = weights / jnp.sum(weights, axis=1, keepdims=True)
            probs[head] = pr
            outs.append(dot(pr.astype(BF16), vd[kv]))
        dp_buf[:, pl.ds(128 * t, 128)] = jnp.where(low_half, outs[0], outs[1]).astype(BF16)
    obuf[...] = dot(dp_buf[:, pl.ds(0, D)], pad_s[...]).astype(BF16)
    att_2[1].end()
    att_2[2].end()
    gain_m = dot(pick14, att_weight(QKV, DP))[0:1]
    for i in range(4):
        cols = pl.ds(256 * i, 256)
        x1[:, cols] = xin[:, cols].astype(F32) + dot(obuf[...], att_weight(QKV + 256 * i, 256))
    middle = x1[...]
    inv2 = lax.rsqrt(jnp.sum(middle * middle, axis=1, keepdims=True) * (1.0 / D) + eps_norm)
    norms[1] = inv2
    unit2 = middle * inv2
    u2[...] = unit2
    h2all[0] = (unit2 * gain_m).astype(BF16)

    def token_sums(part, sums):
        return [
            remote(part.at[1], sums.at[0], device("y", up3(y))),
            remote(part.at[2], sums.at[1], device("y", up1(y))),
            remote(part.at[3], sums.at[2], device("y", up2(y))),
        ]

    def token_total(part, sums, copies):
        for cp in copies:
            cp.wait_recv()
        return part[0].astype(F32) + (
            sums[0].astype(F32) + sums[1].astype(F32) + sums[2].astype(F32))

    def mlp(k, n, need=()):
        rows = n * TOK
        for i in range(5):
            cols, cols_up = pl.ds(256 * i, 256), pl.ds(FP + 256 * i, 256)
            h = h2all[k : k + n].reshape(rows, DP)
            gate = dot(h, w_gu[:, :, :, cols].reshape(DP, 256))
            upward = dot(h, w_gu[:, :, :, cols_up].reshape(DP, 256))
            gact[k : k + n, :, cols] = gate.reshape(n, TOK, 256)
            gact[k : k + n, :, cols_up] = upward.reshape(n, TOK, 256)
            aact[k : k + n, :, cols] = (
                gate * jax.nn.sigmoid(gate) * upward).astype(BF16).reshape(n, TOK, 256)
        for weights in need:
            weights.end()
        for i in range(4):
            cols = pl.ds(256 * i, 256)
            a = aact[k : k + n].reshape(rows, FP)
            part_f[k : k + n, :, cols] = dot(
                a, w_d[:, :, :, cols].reshape(FP, 256)).astype(BF16).reshape(n, TOK, 256)

    ag = TokenGather(h2all, pending)
    sums = token_sums(part_f, sum_f)
    ag.start()

    @pl.when(sec == 1)
    def _():
        dmg.mid()

    gate_z.end()
    up_x.end()

    mlp(0, 1, (low_z, high_x))
    ag.mid()
    mlp(1, 2)
    go(sums[0])
    go(sums[1])
    ag.end()
    mlp(3, 1)
    go(sums[2])
    for c in range(RING):
        cols = pl.ds(128 * c, 128)
        h2t[:, cols] = h2all[c].T
        at[:, cols] = aact[c].T
    h1t[...] = h1[...].T
    ot[...] = obuf[...].T
    out = x1[...] + token_total(part_f, sum_f, sums)
    for cp in pending:
        cp.wait_send()
    pending.clear()
    ybuf[...] = out.astype(BF16)

    @pl.when(sec == 0)
    def _():
        send_y.start()


    def store_states():
        states[...] = dot_back(ybuf[...], pad_s[...]).astype(BF16)

    @pl.when(sec == 0)
    def _():
        store_states()
        send_dx.wait_recv()
        dmall[0] = dyin[...]
        dmg.start()

    def mlp_back(k, n):
        rows = n * TOK
        for i in range(2):
            cols, cols_up = pl.ds(640 * i, 640), pl.ds(FP + 640 * i, 640)
            da = dot_back(dmall[k : k + n].reshape(rows, DP), w_d[2 * i : 2 * i + 2].reshape(640, DP))
            gate = gact[k : k + n, :, cols].reshape(rows, 640)
            upward = gact[k : k + n, :, cols_up].reshape(rows, 640)
            sig = jax.nn.sigmoid(gate)
            dgate = da * upward * (sig * (1.0 + gate * (1.0 - sig)))
            dgu[k : k + n, :, cols] = dgate.astype(BF16).reshape(n, TOK, 640)
            dgu[k : k + n, :, cols_up] = (da * gate * sig).astype(BF16).reshape(n, TOK, 640)
        for i in range(4):
            cols = pl.ds(256 * i, 256)
            part_b[k : k + n, :, cols] = dot_back(
                dgu[k : k + n].reshape(rows, 2 * FP), w_gu[i].reshape(256, 2 * FP)
            ).astype(BF16).reshape(n, TOK, 256)

    sums = token_sums(part_b, sum_b)
    mlp_back(0, 1)

    @pl.when(sec == 0)
    def _():
        dmg.mid()

    mlp_back(1, 2)
    go(sums[0])
    go(sums[1])
    dmg.end()
    mlp_back(3, 1)
    go(sums[2])

    rgate_z = RingReduce(w_gu, lambda c: (c, WHOLE), (0, FP), "z", gu1.at[0], gu2.at[0])
    rup_x = RingReduce(w_gu, lambda c: (WHOLE, c), (FP, 2 * FP), "x", gu1.at[1], gu2.at[1])
    rgate_x = Reduce(w_gu, lambda c: (z, c), (0, FP), "x", gu3.at[0])
    rup_z = Reduce(w_gu, lambda c: (c, x), (FP, 2 * FP), "z", gu3.at[1])
    rlow_z = RingReduce(w_d, lambda c: (WHOLE, c), (0, 512), "z", d1.at[0], d2.at[0])
    rhigh_x = RingReduce(w_d, lambda c: (c, WHOLE), (512, DP), "x", d1.at[1], d2.at[1])
    rlow_x = Reduce(w_d, lambda c: (c, z), (0, 512), "x", d3.at[0])
    rhigh_z = Reduce(w_d, lambda c: (x, c), (512, DP), "z", d3.at[1])
    from_rank = [
        remote(
            w_gu.at[z, x, pl.ds(pl.multiple_of(16 * step(y), 16), 16)],
            gu4.at[y], device("y", step(y)))
        for step in (up1, up3, up2)
    ]
    out_red = [
        Reduce(g_out, reduced("yxz", k), (0, DP), "yxz"[k], r) for k, r in enumerate((out1, out2, out3))]
    qkv_order = ("yxz", "xzy", "zyx")
    qkv_red = [
        [
            Reduce(g_qkv, reduced(order, k), (384 * n, 384 * n + 384), order[k], r.at[n])
            for n, order in enumerate(qkv_order)
        ]
        for k, r in enumerate((qkv1, qkv2, qkv3))
    ]

    def gu_terms():
        def grad_gate(i):
            rows = span(256 * i, 256, 256)
            g = dot(h2t[rows, :], dgu[:, :, pl.ds(0, FP)].reshape(512, FP))
            w_gu[i, :, :, pl.ds(0, FP)] = g.astype(BF16).reshape(4, 64, FP)

        def grad_up(i):
            rows = span(256 * i, 256, 256)
            g = dot(h2t[rows, :], dgu[:, :, pl.ds(FP, FP)].reshape(512, FP))
            w_gu[i, :, :, pl.ds(FP, FP)] = g.astype(BF16).reshape(4, 64, FP)

        times(4, grad_gate)
        rgate_z.start()
        times(4, grad_up)
        rup_x.start()

    def d_terms():
        def grad_d(i):
            rows = span(320 * i, 320, 64)
            g = dot(at[rows, :], dmall[...].reshape(512, DP))
            w_d[i] = g.astype(BF16).reshape(4, 80, DP)

        times(4, grad_d)
        rlow_z.start()
        rhigh_x.start()

    row = lax.rem(lax.broadcasted_iota(jnp.int32, (256, 384), 0), 16)

    def out_terms():
        def grad(i):
            g = dot(ot[span(256 * i, 256, 256), :], datt[...])
            g = jnp.where(row14, dh[0:1, :], g)
            g_out[i] = g.astype(BF16).reshape(4, 4, 16, DP)

        row14 = lax.rem(lax.broadcasted_iota(jnp.int32, (256, DP), 0), 16) == 14
        times(4, grad)
        out_red[0].start()

    gu_terms()

    @pl.when(sec == 0)
    def _():
        d_terms()

    dh2 = token_total(part_b, sum_b, sums)
    unit2 = u2[...]
    dh[0:1, :] = jnp.sum(dh2 * unit2, axis=0, keepdims=True)
    gained = dh2 * gain_m
    dx1 = dyin[...].astype(F32) + norms[1] * (
        gained - unit2 * (jnp.sum(gained * unit2, axis=1, keepdims=True) * (1.0 / D)))
    x1[...] = dx1
    datt[...] = dx1.astype(BF16)

    @pl.when(sec == 0)
    def _():
        out_terms()

    for i in range(4):
        w = w_att[i, :, :, :, pl.ds(QKV, DP)].reshape(256, DP)
        do_buf[:, pl.ds(256 * i, 256)] = dot_back(datt[...], w).astype(BF16)
    proj[:, pl.ds(0, D)] = dot_back(do_buf[...], pad_s[...])

    def unrotated(tile):
        return (tile * cos_t[...] - swap(tile) * sin_t[...]).astype(BF16)

    dk_sum = [jnp.zeros((TOK, 128), F32)] * 2
    dv_sum = [jnp.zeros((TOK, 128), F32)] * 2
    for t in range(7):
        tile = proj[:, pl.ds(128 * t, 128)]
        dqs = []
        for head in (2 * t, 2 * t + 1):
            kv = head // 7
            do_h = jnp.where(keep(head), tile, 0.0).astype(BF16)
            pr = probs[head]
            dpr = dot_back(do_h, vd[kv])
            ds = (pr * (dpr - jnp.sum(dpr * pr, axis=1, keepdims=True))).astype(BF16)
            dv_sum[kv] = dv_sum[kv] + dot_rows(pr.astype(BF16), do_h)
            dk_sum[kv] = dk_sum[kv] + dot_rows(ds, qs[head])
            dqs.append(dot(ds, kd[kv]) * HD ** (-0.5))
        dp_buf[:, pl.ds(128 * t, 128)] = unrotated(jnp.where(low_half, dqs[0], dqs[1]))
    dk_sum = [(dk + pltpu.roll(dk, HD, 1)) * HD ** (-0.5) for dk in dk_sum]
    dv_sum = [dv + pltpu.roll(dv, HD, 1) for dv in dv_sum]
    dp_buf[:, pl.ds(896, 128)] = unrotated(jnp.where(low_half, dk_sum[0], dk_sum[1]))
    dp_buf[:, pl.ds(1024, 128)] = jnp.where(low_half, dv_sum[0], dv_sum[1]).astype(BF16)
    rgate_z.mid()
    rup_x.mid()
    for i in range(4):
        w = w_att[i, :, :, :, pl.ds(0, QKV)].reshape(256, QKV)
        proj[:, pl.ds(256 * i, 256)] = dot_back(dp_buf[...], w)
    dh1 = jnp.where(slot < 14, proj[:, pl.ds(0, DP)], 0.0)
    unit1 = u1[...]
    dgain_a = jnp.sum(dh1 * unit1, axis=0, keepdims=True)

    def qkv_terms():
        proj[0:1, pl.ds(0, DP)] = dgain_a
        for n in range(3):
            cols = pl.ds(384 * n, 384)

            def grad(i, cols=cols):
                g = dot(h1t[span(256 * i, 256, 256), :], dp_buf[:, cols])
                g = jnp.where(row == 15, proj[0:1, cols], g)
                g_qkv[i, :, :, :, cols] = g.astype(BF16).reshape(4, 4, 16, 384)

            times(4, grad)
            qkv_red[0][n].start()

    @pl.when(sec == 0)
    def _():
        qkv_terms()

    gained = dh1 * gain_a
    dx = x1[...] + norms[0] * (
        gained - unit1 * (jnp.sum(gained * unit1, axis=1, keepdims=True) * (1.0 / D)))
    dx_hi = dx.astype(BF16)
    dxbuf[...] = dx_hi

    @pl.when(sec == 1)
    def _():
        send_dx.start()
        igrads[...] = dot_back(dx_hi, pad_s[...])
        d_terms()
        out_terms()
        qkv_terms()
        store_states()

    @pl.when(sec == 0)
    def _():
        dx_lo = (dx - dx_hi.astype(F32)).astype(BF16)
        igrads[...] = dot_back(dx_hi, pad_s[...]) + dot_back(dx_lo, pad_s[...])

    rlow_z.mid()
    rhigh_x.mid()
    rgate_z.end()
    rgate_x.start()
    rup_x.end()
    rup_z.start()
    out_red[0].end()
    out_red[1].start()
    for red, after in zip(qkv_red[0], qkv_red[1]):
        red.end()
        after.start()
    rlow_z.end()
    rlow_x.start()
    rhigh_x.end()
    rhigh_z.start()
    out_red[1].end()
    out_red[2].start()
    rgate_x.end()
    rup_z.end()
    for cp in from_rank:
        go(cp)
    for red, after in zip(qkv_red[1], qkv_red[2]):
        red.end()
        after.start()

    def unpadded(total):
        hi = total.astype(BF16)
        lo = (total - hi.astype(F32)).astype(BF16)
        return dot_back(hi, pad_s[...]) + dot_back(lo, pad_s[...])

    def own_lanes(rows, n):
        width = rows.shape[1]
        target = lax.broadcasted_iota(jnp.int32, (width, 128), 1)
        source = lax.broadcasted_iota(jnp.int32, (width, 128), 0)
        move = jnp.where(source == target + n * me, 1.0, 0.0).astype(BF16)
        hi = rows.astype(BF16)
        lo = (rows - hi.astype(F32)).astype(BF16)
        return dot(hi, move) + dot(lo, move)

    def by_row(ref, rows):
        for r in range(ref.shape[0]):
            ref[r] = rows[r : r + 1]

    by_row(od, unpadded(jnp.concatenate([rlow_x.total(), rhigh_z.total()], axis=1)))
    total = unpadded(out_red[2].total())
    by_row(oout, total)
    ogm[...] = own_lanes(total, 14)[14:15, 0:14]
    for n in range(3):
        proj[0:16, pl.ds(384 * n, 384)] = qkv_red[2][n].total()
    by_row(oqkv, proj[0:16, :])
    ob[...] = own_lanes(proj[0:16, :], 18)[14:15, 0:18]
    oga[...] = own_lanes(proj[0:16, pl.ds(0, DP)], 16)[15:16, 0:14]
    ogate[y] = w_gu[z, x, mine, pl.ds(0, FP)]
    oup[y] = w_gu[z, x, mine, pl.ds(FP, FP)]
    for cp in from_rank:
        cp.wait_recv()
    for step in (up1, up3, up2):
        ogate[step(y)] = gu4[step(y), :, pl.ds(0, FP)]
        oup[step(y)] = gu4[step(y), :, pl.ds(FP, FP)]

    for cp in pending + late:
        cp.wait_send()

    @pl.when(sec == 0)
    def _():
        send_y.wait_send()

    @pl.when(sec == 1)
    def _():
        send_dx.wait_send()


def pad_matrix():
    column = np.arange(DP)
    row = np.where(column % 16 < 14, 14 * (column // 16) + column % 16, -1)
    return (np.arange(D)[:, None] == row[None, :]).astype(jnp.bfloat16)


def frequencies():
    half = HD // 2
    inverse = theta_base ** (-(np.arange(half, dtype=np.float64) * 2.0 / HD))
    sign = np.where(np.arange(128) % HD < half, -1.0, 1.0)
    return np.concatenate([np.tile(inverse, 4)[None], sign[None], np.zeros((6, 128))]).astype(np.float32)


def by_rank(weight):
    pieces = weight.reshape(14, 4, 4, 4, 76).transpose(3, 0, 2, 1, 4)
    return jnp.pad(pieces, ((0, 0), (0, 2), (0, 0), (0, 0), (0, 4))).reshape(4, 16, FP)


def from_rank(grad):
    pieces = grad.reshape(4, 16, 4, 4, 80)[:, :14, :, :, :76]
    return pieces.transpose(1, 3, 2, 0, 4).reshape(1, 14, FF).astype(F32)


def body(
    tokens, segments, cotangent, w_qkv, b_qkv, w_out, gain_attn, gain_mlp, w_gate, w_up, w_down
):
    gu_in = jnp.concatenate([by_rank(w_gate[0]), by_rank(w_up[0])], axis=2)
    vec = jnp.concatenate(
        [jnp.pad(v, ((0, 0), (0, 128 - v.shape[1]))) for v in (b_qkv, gain_attn, gain_mlp)]
        + [jnp.zeros((13, 128), BF16)])
    sds = jax.ShapeDtypeStruct
    vm = pltpu.VMEM
    states, igrads, ogate, oup, od, oqkv, oout, b_grad, ga_grad, gm_grad = pl.pallas_call(
        kernel,
        out_shape=(
            sds((TOK, D), BF16), sds((TOK, D), F32), sds((4, 16, FP), BF16), sds((4, 16, FP), BF16),
            sds((76, 1, D), F32), sds((14, 1, QKV), F32), sds((14, 1, D), F32),
            sds((1, 18), F32), sds((1, 14), F32), sds((1, 14), F32),
        ),
        in_specs=[pl.BlockSpec(memory_space=pltpu.VMEM)] * 10,
        out_specs=tuple([pl.BlockSpec(memory_space=pltpu.VMEM)] * 10),
        scratch_shapes=[
            vm((4, 4, 4, 16, ATT), BF16), vm((4, 4, 64, 2 * FP), BF16), vm((4, 4, 80, DP), BF16),
            vm((4, 4, 4, 16, DP), BF16), vm((4, 4, 4, 16, QKV), BF16),
            *[vm((TOK, DP), BF16)] * 8, vm((TOK, QKV), BF16), vm((DP, TOK), BF16), vm((DP, TOK), BF16),
            vm((4, TOK, DP), BF16), vm((4, TOK, DP), BF16), vm((4, TOK, 2 * FP), F32),
            vm((4, TOK, FP), BF16), vm((4, TOK, 2 * FP), BF16), vm((DP, 512), BF16), vm((FP, 512), BF16),
            vm((4, TOK, DP), BF16), vm((4, TOK, DP), BF16),
            vm((3, TOK, DP), BF16), vm((3, TOK, DP), BF16), vm((8, DP), F32),
            vm((TOK, DP), F32), vm((TOK, DP), F32), vm((TOK, DP), F32), vm((TOK, QKV), F32),
            vm((QH, TOK, 128), BF16), vm((2, TOK, 128), BF16), vm((2, TOK, 128), BF16),
            vm((QH, TOK, 128), F32), vm((2, TOK, 1), F32),
            vm((2, 2, 4, 64, FP // 2), BF16), vm((2, 2, 4, 64, FP), BF16),
            vm((2, 3, 64, FP), BF16), vm((4, 16, 2 * FP), BF16),
            vm((2, 2, 4, 80, 256), BF16), vm((2, 2, 4, 80, 512), BF16), vm((2, 3, 80, 512), BF16),
            vm((3, 4, 4, 16, DP), BF16), vm((3, 4, 16, DP), BF16), vm((3, 16, DP), BF16),
            vm((3, 3, 4, 4, 16, 384), BF16), vm((3, 3, 4, 16, 384), BF16), vm((3, 3, 16, 384), BF16),
            *[vm((TOK, TOK), F32)] * 3,
            pltpu.SemaphoreType.DMA((N_SEM,)), pltpu.SemaphoreType.DMA((N_SEM,)),
            pltpu.SemaphoreType.REGULAR,
        ],
        compiler_params=pltpu.CompilerParams(
            collective_id=0, has_side_effects=True, vmem_limit_bytes=60 * 2**20
        ),
        cost_estimate=pl.CostEstimate(
            flops=15 * 10**9, bytes_accessed=10 * 2**20, transcendentals=2 * 10**6
        ),
    )(
        tokens, cotangent, segments[None], jnp.asarray(frequencies()), gu_in, w_down[0], w_qkv[0], w_out[0], vec,
        jnp.asarray(pad_matrix()),
    )
    rows = lambda array: array.transpose(1, 0, 2)
    return (
        states[None], igrads[None], rows(oqkv), b_grad, rows(oout), ga_grad, gm_grad,
        from_rank(ogate), from_rank(oup), rows(od),
    )


def solution(mesh):
    return jax.shard_map(
        body,
        mesh=mesh,
        in_specs=(
            P("fsdp", None),
            P("fsdp"),
            P("fsdp", None),
            P("section", "fsdp", None),
            P("section", "fsdp"),
            P("section", "fsdp", None),
            P("section", "fsdp"),
            P("section", "fsdp"),
            P("section", "fsdp", None),
            P("section", "fsdp", None),
            P("section", "fsdp", None),
        ),
        out_specs=(
            P("section", "fsdp", None),
            P("section", "fsdp", None),
            P("section", "fsdp", None),
            P("section", "fsdp"),
            P("section", "fsdp", None),
            P("section", "fsdp"),
            P("section", "fsdp"),
            P("section", "fsdp", None),
            P("section", "fsdp", None),
            P("section", "fsdp", None),
        ),
        check_vma=False,
    )
```
